128 devices in a mesh: row: 8 (over x, core), col: 16 (over y, z).
Axes of the slice: x: 4, y: 4, z: 4, core: 2. Of those that a mesh axis runs over, the one named last changes fastest.
Arguments:
- orbitals: float32 [512, 32, 1024], P(('row', 'col')), may hold values from -6 to 6
- gradient: float32 [512, 32, 1024], P(('row', 'col')), may hold values from -4 to 4
- offsets: int32 [512, 3], replicated, may hold values from 0 to 3
- pairs: int32 [128, 4, 2], P('row'), may hold values from 0 to 511, as said below
- counts: int32 [128], P('row'), may hold values from 1 to 4, as said below
Outputs:
- updated: float32 [512, 32, 1024], P(('row', 'col'))
- energies: float32 [2], replicated
The draws below stay inside these ranges and needn't reach their ends.
Inputs may be any that keep to these rules, and one draw needn't show every extreme that they name: `pairs`: both orbitals of a slot of pair owner p belong to p's group, ids g * 64 to (g + 1) * 64 - 1 with g = p // 16 (device d owns ids d * 4 onward). Among the live slots of one pair owner at most 2 distinct orbitals come from any one device, and every owner reaches 2 from some device. `counts`: every group of 16 pair owners has one owner with 4 live slots.
All inputs are finite; a program needn't handle non-finite values.
Results may differ from the reference program's by a relative error of at most 0.0082.
Values may be sent and summed in bfloat16 or wider, within the bound.
A program may use at most 64 MiB of HBM per device.

```python
import jax
import jax.numpy as jnp
from jax import lax

BOX = 32
ORB_DEV = 4
PAIR_DEV = 4
CAP = 2
SHIFT = 4
SWEEPS = 12
ROUNDS = 2
GROUP_ORB = 64
NORB = 512
OWNERS = 128
N_ROW = 8
N_COL = 16


def draw_pairs(key, part):
    columns = GROUP_ORB // ORB_DEV
    pick_key = jax.random.fold_in(key, 11)
    slot_key = jax.random.fold_in(key, 12)
    source_key = jax.random.fold_in(key, 13)
    scores = jax.random.randint(pick_key, (OWNERS, columns, ORB_DEV), 0, 1 << 20) * ORB_DEV + jnp.arange(ORB_DEV)
    chosen = jnp.argsort(scores, axis=-1)[..., :CAP]
    candidates = (jnp.arange(columns)[None, :, None] * ORB_DEV + chosen).reshape(OWNERS, columns * CAP)
    picks = jax.random.randint(slot_key, (OWNERS, PAIR_DEV, 2), 0, columns * CAP)
    anchor = jax.random.randint(source_key, (OWNERS,), 0, columns) * CAP
    picks = picks.at[:, 0, 0].set(anchor).at[:, 0, 1].set(anchor + 1)
    local = jnp.take_along_axis(candidates, picks.reshape(OWNERS, PAIR_DEV * 2), axis=1).reshape(OWNERS, PAIR_DEV, 2)
    group_base = jnp.arange(OWNERS) // columns * GROUP_ORB
    return (local + group_base[:, None, None]).astype(jnp.int32)


def draw_counts(key, part):
    columns = GROUP_ORB // ORB_DEV
    groups = NORB // GROUP_ORB
    base_key = jax.random.fold_in(key, 21)
    full_key = jax.random.fold_in(key, 22)
    drawn = jax.random.randint(base_key, (OWNERS,), 1, PAIR_DEV // 2 + 1)
    busiest = jnp.arange(groups) * columns + jax.random.randint(full_key, (groups,), 0, columns)
    return drawn.at[busiest].set(PAIR_DEV).astype(jnp.int32)


def with_ends(values, own_key, least, high):
    shape = values.shape
    index_at = [jax.random.randint(jax.random.fold_in(own_key, axis), (), 0, shape[axis]) for axis in range(len(shape))]
    values = values.at[tuple(index_at)].set(least)
    longest = shape.index(max(shape))
    index_at[longest] = (index_at[longest] + 1) % shape[longest]
    return values.at[tuple(index_at)].set(high)


def shard_levels(own_key, dims, pieces, low, largest):
    factor_of, own = 1.0, jax.random.fold_in(own_key, 6)
    for dim, shards_of in pieces:
        draws = jnp.exp(jax.random.uniform(jax.random.fold_in(own, dim), (shards_of,), jnp.float32, low / len(pieces), largest / len(pieces)))
        factor_of = factor_of * jnp.repeat(draws, dims[dim] // shards_of).reshape([-1 if axis == dim else 1 for axis in range(len(dims))])
    return factor_of


def centred(rng, dims, width, most, split=(), kind=jnp.bfloat16):
    values = jax.random.normal(rng, dims, jnp.float32) * width
    if len(split) > 0:
        values = shard_levels(rng, dims, split, -0.22, 0.18) * values
    return jnp.clip(values, min=-most, max=most).astype(kind)


def setup_inputs(seed: int = 0) -> dict:
    splits = jax.random.split(jax.random.key(seed), 6)
    orbitals = centred(splits[0], (NORB, BOX, BOX * BOX), 1.0, 6.0, ((0, 128),), jnp.float32)
    gradient = centred(splits[1], (NORB, BOX, BOX * BOX), 0.5, 4.0, ((0, 128),), jnp.float32)
    offsets = with_ends(jax.random.randint(splits[2], (NORB, 3), 0, SHIFT), jax.random.fold_in(splits[2], 1), 0, SHIFT - 1).astype(jnp.int32)
    pairs = draw_pairs(jax.random.fold_in(splits[5], 71), 0)
    counts = draw_counts(jax.random.fold_in(splits[5], 71), 0)
    return dict(orbitals=orbitals, gradient=gradient, offsets=offsets, pairs=pairs, counts=counts)


screen_mu = 0.1
damping = 0.5


def sweep_table(sweeps):
    center_val = 6.0 + screen_mu
    half_width = 6.0
    ratio_val = center_val / half_width
    prev_coef = 1.0 / ratio_val
    keep_list = []
    mix_list = []
    for sweep_idx in range(sweeps):
        next_coef = 1.0 / (2.0 * ratio_val - prev_coef)
        keep_list.append(next_coef * prev_coef)
        mix_list.append(2.0 * next_coef / half_width)
        prev_coef = next_coef
    return jnp.array(keep_list, jnp.float32), jnp.array(mix_list, jnp.float32), 1.0 / center_val


def apply_operator(field):
    edge = field.shape[0]
    plane = field.shape[1]
    zero_row = jnp.zeros_like(field[:1])
    along_x = jnp.concatenate([field[1:], zero_row], 0) + jnp.concatenate([zero_row, field[:-1]], 0)
    zero_band = jnp.zeros_like(field[:, :edge])
    along_y = jnp.concatenate([field[:, edge:], zero_band], 1) + jnp.concatenate([zero_band, field[:, :-edge]], 1)
    zero_col = jnp.zeros_like(field[:, :1])
    depth = jnp.arange(plane) % edge
    upper = jnp.where(depth < edge - 1, jnp.concatenate([field[:, 1:], zero_col], 1), 0.0)
    lower = jnp.where(depth > 0, jnp.concatenate([zero_col, field[:, :-1]], 1), 0.0)
    return (6.0 + screen_mu) * field - (along_x + along_y + upper + lower)


def screened_solve(source, tables):
    keep_coef, mix_coef, first_coef = tables

    def sweep(index, state):
        solution, remainder, direction = state
        solution = solution + direction
        remainder = remainder - apply_operator(direction)
        direction = keep_coef[index] * direction + mix_coef[index] * remainder
        return solution, remainder, direction

    state = (jnp.zeros_like(source), source, source * first_coef)
    return lax.fori_loop(0, keep_coef.shape[0], sweep, state)[0]


def displaced(box, shift):
    edge = box.shape[0]
    reach = SHIFT - 1
    cube = jnp.pad(box.reshape(edge, edge, edge), reach)
    start = (shift + reach).astype(jnp.int32)
    moved = lax.dynamic_slice(cube, (start[0], start[1], start[2]), (edge, edge, edge))
    return moved.reshape(edge, edge * edge)


def run_pairs(boxes, source_of, slot_of, mine, mine_count, group_offsets, tables, slots):
    edge = boxes.shape[1]
    plane = boxes.shape[2]
    collected = jnp.zeros((slots, edge, plane), jnp.float32)

    def one_pair(index, state):
        gathered, energy = state
        first = mine[index, 0]
        second = mine[index, 1]
        shift = group_offsets[first] - group_offsets[second]
        box_i = lax.dynamic_index_in_dim(boxes, source_of[first], 0, False).astype(jnp.float32)
        box_j = displaced(lax.dynamic_index_in_dim(boxes, source_of[second], 0, False), shift).astype(jnp.float32)
        density = box_i * box_j
        potential = screened_solve(density, tables)
        term = potential * box_j
        target = slot_of[first]
        current = lax.dynamic_index_in_dim(gathered, target, 0, False)
        gathered = lax.dynamic_update_index_in_dim(gathered, current + term, target, 0)
        return gathered, energy + jnp.sum(density * potential)

    return lax.fori_loop(0, mine_count, one_pair, (collected, jnp.zeros((), jnp.float32)))


def reference(orbitals, gradient, offsets, pairs, counts):
    tables = sweep_table(SWEEPS)
    group = N_COL * ORB_DEV
    owners = N_ROW * N_COL
    orbit_ids = jnp.arange(group, dtype=jnp.int32)
    current = orbitals
    totals = []
    for round_idx in range(ROUNDS):
        boxes_all = current.astype(jnp.bfloat16)

        def per_owner(state, owner):
            field, energy = state
            base = ((owner // N_COL) * group).astype(jnp.int32)
            boxes = lax.dynamic_slice_in_dim(boxes_all, base, group, 0)
            group_offsets = lax.dynamic_slice_in_dim(offsets, base, group, 0)
            mine = (pairs[owner] - base).astype(jnp.int32)
            gathered, pair_energy = run_pairs(boxes, orbit_ids, orbit_ids, mine, counts[owner], group_offsets, tables, group)
            rounded = lax.optimization_barrier(gathered.astype(jnp.bfloat16)).astype(jnp.float32)
            previous = lax.dynamic_slice_in_dim(field, base, group, 0)
            field = lax.dynamic_update_slice_in_dim(field, previous + rounded, base, 0)
            return (field, energy + pair_energy), None

        start_state = (jnp.zeros_like(current), jnp.zeros((), jnp.float32))
        (field, energy), unused = lax.scan(per_owner, start_state, jnp.arange(owners, dtype=jnp.int32))
        totals.append(energy)
        current = current - damping * (gradient + field)
    energies = jnp.stack(totals) / (BOX * BOX * BOX * owners)
    return current, energies
```

```python
import functools

import jax
import jax.numpy as jnp
import ml_dtypes
import numpy as np
from jax import lax
from jax.experimental import pallas as pl
from jax.experimental.pallas import tpu as pltpu
from jax.sharding import PartitionSpec as P

SWEEPS = 12
ROUNDS = 2
TILE_R = 16
TILE_C = 128
screen_mu = 0.1
damping = 0.5


def spectral_tables(edge):
    k = np.arange(1, edge + 1)
    basis = np.sqrt(2.0 / (edge + 1)) * np.sin(np.pi * np.outer(k, k) / (edge + 1))
    line = 2.0 * np.cos(np.pi * k / (edge + 1))
    eig = (6.0 + screen_mu) - (line[:, None, None] + line[None, :, None] + line[None, None, :])
    c, h = 6.0 + screen_mu, 6.0
    g = c / h
    q = 1.0 / g
    u = np.zeros_like(eig)
    t = np.ones_like(eig)
    d = t / c
    for _ in range(SWEEPS):
        u = u + d
        t = t - eig * d
        q_new = 1.0 / (2.0 * g - q)
        d = q_new * q * d + (2.0 * q_new / h) * t
        q = q_new
    return basis, u.reshape(edge, edge * edge)


def two_parts(x):
    high = x.astype(ml_dtypes.bfloat16)
    return np.stack([high, (x - high.astype(np.float64)).astype(ml_dtypes.bfloat16)])


def split(x):
    high = x.astype(jnp.bfloat16)
    return high, (x - high.astype(jnp.float32)).astype(jnp.bfloat16)


def dot(a, b):
    return jnp.dot(a, b, preferred_element_type=jnp.float32)


def dot_split(a, b):
    (a_high, a_low), (b_high, b_low) = a, b
    return dot(a_high, b_high) + (dot(a_low, b_high) + dot(a_high, b_low))


def peers(n_col):
    side = int(round(n_col**0.5))
    steps = [(a, b) for a in range(side) for b in range(side) if a + b > 0]
    return side, sorted(steps, key=lambda p: -(min(p[0], side - p[0]) + min(p[1], side - p[1])))


def kernel(
    n_row,
    n_col,
    S,
    tbl,
    orb_hbm,
    grad_hbm,
    kron_hbm,
    sx_hbm,
    poly_hbm,
    exb,
    energy_out,
    orb,
    grad,
    kron,
    sx,
    poly,
    box_stage,
    q_stage,
    slab0,
    q_slab,
    slab1,
    pack,
    pair_box,
    partner,
    density,
    term_stage,
    terms,
    wide,
    summed,
    final_stage,
    e_mine,
    e_group,
    e_sum,
    e_row,
    first_of,
    second_of,
    load_sem,
    send_sem,
    recv_sem,
):
    me = lax.axis_index("col")
    row = lax.axis_index("row")
    own, edge, plane = orb.shape
    norb = own * n_col
    slots = S * n_col
    halves = edge // TILE_R
    strips = plane // TILE_C

    loads = [
        pltpu.make_async_copy(a, b, load_sem.at[i])
        for i, (a, b) in enumerate(
            ((orb_hbm, orb), (grad_hbm, grad), (kron_hbm, kron), (sx_hbm, sx), (poly_hbm, poly))
        )
    ]
    for one in loads:
        one.start()

    barrier = pltpu.get_barrier_semaphore()

    def greet_col(d, _):
        pl.semaphore_signal(barrier, inc=1, device_id={"col": (me + d) % n_col}, device_id_type=pl.DeviceIdType.MESH)
        return 0

    def greet_row(d, _):
        pl.semaphore_signal(barrier, inc=1, device_id={"row": (row + d) % n_row}, device_id_type=pl.DeviceIdType.MESH)
        return 0

    lax.fori_loop(1, n_col, greet_col, 0)
    lax.fori_loop(1, n_row, greet_row, 0)

    count_at = n_col * 8
    offset_at = count_at + n_col

    def rank(r, firsts):
        def seek(p, state):
            start, found = state
            count = tbl[count_at + p]
            inside = (r >= start) & (r < start + count)
            return start + count, jnp.where(inside, p * 4 + r - start, found)

        total, found = lax.fori_loop(0, n_col, seek, (jnp.int32(0), jnp.int32(-1)))
        at = jnp.maximum(found, 0) * 2
        first = tbl[at]
        first_of[r] = first
        second_of[r] = tbl[at + 1]
        lane = lax.broadcasted_iota(jnp.int32, (norb, slots), 1)
        return jnp.where(lane == r, jnp.where(found >= 0, first, -1), firsts)

    firsts = lax.fori_loop(0, slots, rank, jnp.full((norb, slots), -1, jnp.int32))
    choose = (lax.broadcasted_iota(jnp.int32, (norb, slots), 0) == firsts).astype(jnp.float32).astype(jnp.bfloat16)

    def total_live(p, acc):
        return acc + tbl[count_at + p]

    live_total = lax.fori_loop(0, n_col, total_live, jnp.int32(0))

    def tile_of(s):
        return pl.ds(pl.multiple_of((s // strips) * TILE_R, TILE_R), TILE_R), pl.ds(
            pl.multiple_of((s % strips) * TILE_C, TILE_C), TILE_C
        )

    my_rows, my_cols = tile_of(me)

    def exchange(src_of, dst, which, before=None):
        side, steps = peers(n_col)
        for dy, dz in steps:
            to = ((me // side + dy) % side) * side + (me % side + dz) % side
            if before is not None:
                before(to)
            pltpu.make_async_remote_copy(
                src_ref=src_of(to),
                dst_ref=dst,
                send_sem=send_sem.at[which],
                recv_sem=recv_sem.at[which],
                device_id={"col": to},
                device_id_type=pl.DeviceIdType.MESH,
            ).start()
        if before is not None:
            before(me)
        pltpu.make_async_copy(src_of(me), dst, recv_sem.at[which]).start()

    def arrived(ref, which):
        pltpu.make_async_copy(ref, ref, recv_sem.at[which]).wait()

    def sent(ref, which):
        pltpu.make_async_copy(ref, ref, send_sem.at[which]).wait()

    loads[0].wait()
    box_stage[...] = orb[...].astype(jnp.bfloat16)
    pl.semaphore_wait(barrier, n_col - 1 + n_row - 1)

    def from_boxes(s):
        rows, cols = tile_of(s)
        return box_stage.at[:, rows, cols]

    def from_q(s):
        rows, cols = tile_of(s)
        return q_stage.at[:, rows, cols]

    mine4 = pl.ds(me * own, own)
    exchange(from_boxes, slab0.at[mine4], 0)
    loads[1].wait()
    q_stage[...] = orb[...] - damping * grad[...]
    exchange(from_q, q_slab.at[mine4], 1)
    for one in loads[2:]:
        one.wait()

    energies = []
    for r in range(ROUNDS):
        slab = (slab0, slab1)[r]
        if r == 0:
            arrived(slab0, 0)

        def fill(p):
            for k in range(S):
                pack[r, p * 2 * S + 2 * k] = slab[first_of[p * S + k]]
                pack[r, p * 2 * S + 2 * k + 1] = slab[second_of[p * S + k]]

        def from_pack(p):
            return pack.at[r, pl.ds(p * 2 * S, 2 * S)]

        exchange(from_pack, pair_box.at[r, :, my_rows, my_cols], 2 + 2 * r, fill)
        arrived(pair_box.at[r], 2 + 2 * r)

        lane = lax.broadcasted_iota(jnp.int32, (edge, plane), 1)
        line = lax.broadcasted_iota(jnp.int32, (edge, plane), 0)
        for k in range(S):
            a = offset_at + 3 * first_of[me * S + k]
            b = offset_at + 3 * second_of[me * S + k]
            dx = tbl[a] - tbl[b]
            dy = tbl[a + 1] - tbl[b + 1]
            dz = tbl[a + 2] - tbl[b + 2]
            t = dy * edge + dz
            moved = pair_box[r, 2 * k + 1].astype(jnp.float32)
            moved = pltpu.roll(moved, lax.rem(plane - t, jnp.int32(plane)), 1)
            moved = pltpu.roll(moved, lax.rem(edge - dx, jnp.int32(edge)), 0)
            at_x = line + dx
            at_y = lane // edge + dy
            at_z = lane % edge + dz
            inside = (
                (at_x >= 0) & (at_x < edge) & (at_y >= 0) & (at_y < edge) & (at_z >= 0) & (at_z < edge)
            )
            moved = jnp.where(inside, moved, 0.0)
            partner[pl.ds(k * edge, edge), :] = moved
            density[pl.ds(k * edge, edge), :] = pair_box[r, 2 * k].astype(jnp.float32) * moved

        yz = kron[0], kron[1]
        along_x = sx[0], sx[1]
        modes = dot_split(split(density[...]), yz)
        modes = dot_split(along_x, split(modes)).reshape(S, edge, plane) * poly[...][None]
        modes = dot_split(along_x, split(modes.reshape(S * edge, plane)))
        potential = dot_split(split(modes), yz)
        term_stage[r] = (potential * partner[...]).astype(jnp.bfloat16).reshape(S, edge, plane)
        cells = (density[...] * potential).reshape(S, edge, plane)
        energy = jnp.zeros((edge, plane), jnp.float32)
        for k in range(S):
            energy = energy + jnp.where(me * S + k < live_total, cells[k], 0.0)
        energies.append(energy)

        def from_terms(s):
            rows, cols = tile_of(s)
            return term_stage.at[r, :, rows, cols]

        exchange(from_terms, terms.at[r, pl.ds(me * S, S)], 3 + 2 * r)

        if r == ROUNDS - 1:
            for i, e in enumerate(energies):
                part = jnp.sum(e.reshape(edge // 8, 8, plane), axis=0)
                e_mine[i] = sum(part[:, c * TILE_C : (c + 1) * TILE_C] for c in range(strips))
            exchange(lambda s: e_mine, e_group.at[me], 7)

        arrived(terms.at[r], 3 + 2 * r)
        wide[...] = terms[r].astype(jnp.float32).reshape(slots * TILE_R, TILE_C)
        if r == 0:
            arrived(q_slab, 1)
        for j in range(TILE_R):
            part = wide[pl.ds(j, slots, stride=TILE_R), :].astype(jnp.bfloat16)
            out = dot(choose, part)
            if r == 0:
                summed[pl.ds(j, norb, stride=TILE_R), :] = out
            else:
                summed[pl.ds(j, norb, stride=TILE_R), :] += out
        if r == 0:
            total = summed[...].reshape(norb, TILE_R, TILE_C)
            slab1[...] = (q_slab[...] - damping * total).astype(jnp.bfloat16)
        else:
            final_stage[...] = summed[...].reshape(norb, TILE_R, TILE_C).astype(jnp.bfloat16)

    exchange(lambda s: final_stage.at[pl.ds(s * own, own)], exb.at[:, my_rows, my_cols], 6)

    arrived(e_group, 7)
    e_sum[...] = jnp.sum(e_group[...], axis=0)

    def go_row(d, _):
        pltpu.make_async_remote_copy(
            src_ref=e_sum,
            dst_ref=e_row.at[row],
            send_sem=send_sem.at[8],
            recv_sem=recv_sem.at[8],
            device_id={"row": (row + d) % n_row},
            device_id_type=pl.DeviceIdType.MESH,
        ).start()
        return 0

    lax.fori_loop(1, n_row, go_row, 0)
    pltpu.make_async_copy(e_sum, e_row.at[row], recv_sem.at[8]).start()
    arrived(e_row, 8)
    all_cells = edge * edge * edge * n_row * n_col
    for i in range(ROUNDS):
        energy_out[i] = jnp.sum(jnp.sum(e_row[:, i], axis=0)) / all_cells
    arrived(exb, 6)

    others = n_col - 1
    sent(slab0.at[pl.ds(0, others * own)], 0)
    sent(q_slab.at[pl.ds(0, others * own)], 1)
    for r in range(ROUNDS):
        sent(pack.at[r, pl.ds(0, others * 2 * S)], 2 + 2 * r)
        sent(terms.at[r, pl.ds(0, others * S)], 3 + 2 * r)
    sent(final_stage.at[pl.ds(0, others * own)], 6)
    sent(e_group.at[pl.ds(0, others)], 7)
    if n_row > 1:
        sent(e_row.at[pl.ds(0, n_row - 1)], 8)


def local(n_row, n_col, S, orbitals, gradient, offsets, pairs, counts):
    own, edge, plane = orbitals.shape
    norb = own * n_col
    slots = S * n_col
    base = lax.axis_index("row") * norb
    table = jnp.concatenate(
        [
            (pairs - base).reshape(-1),
            counts,
            lax.dynamic_slice_in_dim(offsets, base, norb, 0).reshape(-1),
        ]
    )
    basis, poly = spectral_tables(edge)
    kron = two_parts(np.kron(basis, basis))
    sx = two_parts(np.kron(np.eye(S), basis))
    hbm = pl.BlockSpec(memory_space=pltpu.HBM)
    f32, bf16 = jnp.float32, jnp.bfloat16
    tiles = (norb, TILE_R, TILE_C)
    exchanged, energies = pl.pallas_call(
        functools.partial(kernel, n_row, n_col, S),
        out_shape=(
            jax.ShapeDtypeStruct((own, edge, plane), bf16),
            jax.ShapeDtypeStruct((ROUNDS,), f32),
        ),
        in_specs=[pl.BlockSpec(memory_space=pltpu.SMEM)] + [hbm] * 5,
        out_specs=(pl.BlockSpec(memory_space=pltpu.VMEM), pl.BlockSpec(memory_space=pltpu.SMEM)),
        scratch_shapes=[
            pltpu.VMEM((own, edge, plane), f32),
            pltpu.VMEM((own, edge, plane), f32),
            pltpu.VMEM((2, plane, plane), bf16),
            pltpu.VMEM((2, S * edge, S * edge), bf16),
            pltpu.VMEM((edge, plane), f32),
            pltpu.VMEM((own, edge, plane), bf16),
            pltpu.VMEM((own, edge, plane), f32),
            pltpu.VMEM(tiles, bf16),
            pltpu.VMEM(tiles, f32),
            pltpu.VMEM(tiles, bf16),
            pltpu.VMEM((ROUNDS, slots * 2, TILE_R, TILE_C), bf16),
            pltpu.VMEM((ROUNDS, 2 * S, edge, plane), bf16),
            pltpu.VMEM((S * edge, plane), f32),
            pltpu.VMEM((S * edge, plane), f32),
            pltpu.VMEM((ROUNDS, S, edge, plane), bf16),
            pltpu.VMEM((ROUNDS, slots, TILE_R, TILE_C), bf16),
            pltpu.VMEM((slots * TILE_R, TILE_C), f32),
            pltpu.VMEM((norb * TILE_R, TILE_C), f32),
            pltpu.VMEM(tiles, bf16),
            pltpu.VMEM((ROUNDS, 8, TILE_C), f32),
            pltpu.VMEM((n_col, ROUNDS, 8, TILE_C), f32),
            pltpu.VMEM((ROUNDS, 8, TILE_C), f32),
            pltpu.VMEM((n_row, ROUNDS, 8, TILE_C), f32),
            pltpu.SMEM((slots,), jnp.int32),
            pltpu.SMEM((slots,), jnp.int32),
            pltpu.SemaphoreType.DMA((5,)),
            pltpu.SemaphoreType.DMA((9,)),
            pltpu.SemaphoreType.DMA((9,)),
        ],
        compiler_params=pltpu.CompilerParams(
            collective_id=S, has_side_effects=True, vmem_limit_bytes=60 * 1024 * 1024
        ),
    )(table, orbitals, gradient, jnp.asarray(kron), jnp.asarray(sx), jnp.asarray(poly.astype(np.float32)))
    updated = orbitals - gradient - damping * exchanged.astype(f32)
    return updated, energies


def solution(mesh):
    n_row, n_col = mesh.shape["row"], mesh.shape["col"]
    both = P(("row", "col"), None, None)
    return jax.shard_map(
        functools.partial(local, n_row, n_col, 4),
        mesh=mesh,
        in_specs=(both, both, P(), P("row", None, None), P("row")),
        out_specs=(both, P()),
        check_vma=False,
    )
```

```python
import functools

import jax
import jax.numpy as jnp
import ml_dtypes
import numpy as np
from jax import lax
from jax.experimental import pallas as pl
from jax.experimental.pallas import tpu as pltpu
from jax.sharding import PartitionSpec as P

SWEEPS = 12
ROUNDS = 2
TILE_R = 16
TILE_C = 128
screen_mu = 0.1
damping = 0.5


def spectral_tables(edge):
    k = np.arange(1, edge + 1)
    basis = np.sqrt(2.0 / (edge + 1)) * np.sin(np.pi * np.outer(k, k) / (edge + 1))
    line = 2.0 * np.cos(np.pi * k / (edge + 1))
    eig = (6.0 + screen_mu) - (line[:, None, None] + line[None, :, None] + line[None, None, :])
    c, h = 6.0 + screen_mu, 6.0
    g = c / h
    q = 1.0 / g
    u = np.zeros_like(eig)
    t = np.ones_like(eig)
    d = t / c
    for _ in range(SWEEPS):
        u = u + d
        t = t - eig * d
        q_new = 1.0 / (2.0 * g - q)
        d = q_new * q * d + (2.0 * q_new / h) * t
        q = q_new
    return basis, u.reshape(edge, edge * edge)


def two_parts(x):
    high = x.astype(ml_dtypes.bfloat16)
    return np.stack([high, (x - high.astype(np.float64)).astype(ml_dtypes.bfloat16)])


def split(x):
    high = x.astype(jnp.bfloat16)
    return high, (x - high.astype(jnp.float32)).astype(jnp.bfloat16)


def dot(a, b):
    return jnp.dot(a, b, preferred_element_type=jnp.float32)


def dot_split(a, b):
    (a_high, a_low), (b_high, b_low) = a, b
    return dot(a_high, b_high) + (dot(a_low, b_high) + dot(a_high, b_low))


def peers(n_col):
    side = int(round(n_col**0.5))
    steps = [(a, b) for a in range(side) for b in range(side) if a + b > 0]
    return side, sorted(steps, key=lambda p: -(min(p[0], side - p[0]) + min(p[1], side - p[1])))


def spread_kernel(
    n_row,
    n_col,
    S,
    tbl,
    orb_hbm,
    grad_hbm,
    kron_hbm,
    sx_hbm,
    poly_hbm,
    exb,
    energy_out,
    orb,
    grad,
    kron,
    sx,
    poly,
    box_stage,
    q_stage,
    slab0,
    q_slab,
    slab1,
    pack,
    pair_box,
    partner,
    density,
    term_stage,
    terms,
    wide,
    summed,
    final_stage,
    e_mine,
    e_group,
    e_sum,
    e_row,
    first_of,
    second_of,
    load_sem,
    send_sem,
    recv_sem,
):
    me = lax.axis_index("col")
    row = lax.axis_index("row")
    own, edge, plane = orb.shape
    norb = own * n_col
    slots = S * n_col
    halves = edge // TILE_R
    strips = plane // TILE_C

    loads = [
        pltpu.make_async_copy(a, b, load_sem.at[i])
        for i, (a, b) in enumerate(
            ((orb_hbm, orb), (grad_hbm, grad), (kron_hbm, kron), (sx_hbm, sx), (poly_hbm, poly))
        )
    ]
    for one in loads:
        one.start()

    barrier = pltpu.get_barrier_semaphore()

    def greet_col(d, _):
        pl.semaphore_signal(barrier, inc=1, device_id={"col": (me + d) % n_col}, device_id_type=pl.DeviceIdType.MESH)
        return 0

    def greet_row(d, _):
        pl.semaphore_signal(barrier, inc=1, device_id={"row": (row + d) % n_row}, device_id_type=pl.DeviceIdType.MESH)
        return 0

    lax.fori_loop(1, n_col, greet_col, 0)
    lax.fori_loop(1, n_row, greet_row, 0)

    count_at = n_col * 8
    offset_at = count_at + n_col

    def rank(r, firsts):
        def seek(p, state):
            start, found = state
            count = tbl[count_at + p]
            inside = (r >= start) & (r < start + count)
            return start + count, jnp.where(inside, p * 4 + r - start, found)

        total, found = lax.fori_loop(0, n_col, seek, (jnp.int32(0), jnp.int32(-1)))
        at = jnp.maximum(found, 0) * 2
        first = tbl[at]
        first_of[r] = first
        second_of[r] = tbl[at + 1]
        lane = lax.broadcasted_iota(jnp.int32, (norb, slots), 1)
        return jnp.where(lane == r, jnp.where(found >= 0, first, -1), firsts)

    firsts = lax.fori_loop(0, slots, rank, jnp.full((norb, slots), -1, jnp.int32))
    choose = (lax.broadcasted_iota(jnp.int32, (norb, slots), 0) == firsts).astype(jnp.float32).astype(jnp.bfloat16)

    def total_live(p, acc):
        return acc + tbl[count_at + p]

    live_total = lax.fori_loop(0, n_col, total_live, jnp.int32(0))

    def tile_of(s):
        return pl.ds(pl.multiple_of((s // strips) * TILE_R, TILE_R), TILE_R), pl.ds(
            pl.multiple_of((s % strips) * TILE_C, TILE_C), TILE_C
        )

    my_rows, my_cols = tile_of(me)

    def exchange(src_of, dst, which, before=None):
        side, steps = peers(n_col)
        for dy, dz in steps:
            to = ((me // side + dy) % side) * side + (me % side + dz) % side
            if before is not None:
                before(to)
            pltpu.make_async_remote_copy(
                src_ref=src_of(to),
                dst_ref=dst,
                send_sem=send_sem.at[which],
                recv_sem=recv_sem.at[which],
                device_id={"col": to},
                device_id_type=pl.DeviceIdType.MESH,
            ).start()
        if before is not None:
            before(me)
        pltpu.make_async_copy(src_of(me), dst, recv_sem.at[which]).start()

    def arrived(ref, which):
        pltpu.make_async_copy(ref, ref, recv_sem.at[which]).wait()

    def sent(ref, which):
        pltpu.make_async_copy(ref, ref, send_sem.at[which]).wait()

    loads[0].wait()
    box_stage[...] = orb[...].astype(jnp.bfloat16)
    pl.semaphore_wait(barrier, n_col - 1 + n_row - 1)

    def from_boxes(s):
        rows, cols = tile_of(s)
        return box_stage.at[:, rows, cols]

    def from_q(s):
        rows, cols = tile_of(s)
        return q_stage.at[:, rows, cols]

    mine4 = pl.ds(me * own, own)
    exchange(from_boxes, slab0.at[mine4], 0)
    loads[1].wait()
    q_stage[...] = orb[...] - damping * grad[...]
    exchange(from_q, q_slab.at[mine4], 1)
    for one in loads[2:]:
        one.wait()

    energies = []
    for r in range(ROUNDS):
        slab = (slab0, slab1)[r]
        if r == 0:
            arrived(slab0, 0)

        def fill(p):
            for k in range(S):
                pack[r, p * 2 * S + 2 * k] = slab[first_of[p * S + k]]
                pack[r, p * 2 * S + 2 * k + 1] = slab[second_of[p * S + k]]

        def from_pack(p):
            return pack.at[r, pl.ds(p * 2 * S, 2 * S)]

        exchange(from_pack, pair_box.at[r, :, my_rows, my_cols], 2 + 2 * r, fill)
        arrived(pair_box.at[r], 2 + 2 * r)

        lane = lax.broadcasted_iota(jnp.int32, (edge, plane), 1)
        line = lax.broadcasted_iota(jnp.int32, (edge, plane), 0)
        for k in range(S):
            a = offset_at + 3 * first_of[me * S + k]
            b = offset_at + 3 * second_of[me * S + k]
            dx = tbl[a] - tbl[b]
            dy = tbl[a + 1] - tbl[b + 1]
            dz = tbl[a + 2] - tbl[b + 2]
            t = dy * edge + dz
            moved = pair_box[r, 2 * k + 1].astype(jnp.float32)
            moved = pltpu.roll(moved, lax.rem(plane - t, jnp.int32(plane)), 1)
            moved = pltpu.roll(moved, lax.rem(edge - dx, jnp.int32(edge)), 0)
            at_x = line + dx
            at_y = lane // edge + dy
            at_z = lane % edge + dz
            inside = (
                (at_x >= 0) & (at_x < edge) & (at_y >= 0) & (at_y < edge) & (at_z >= 0) & (at_z < edge)
            )
            moved = jnp.where(inside, moved, 0.0)
            partner[pl.ds(k * edge, edge), :] = moved
            density[pl.ds(k * edge, edge), :] = pair_box[r, 2 * k].astype(jnp.float32) * moved

        yz = kron[0], kron[1]
        along_x = sx[0], sx[1]
        modes = dot_split(split(density[...]), yz)
        modes = dot_split(along_x, split(modes)).reshape(S, edge, plane) * poly[...][None]
        modes = dot_split(along_x, split(modes.reshape(S * edge, plane)))
        potential = dot_split(split(modes), yz)
        term_stage[r] = (potential * partner[...]).astype(jnp.bfloat16).reshape(S, edge, plane)
        cells = (density[...] * potential).reshape(S, edge, plane)
        energy = jnp.zeros((edge, plane), jnp.float32)
        for k in range(S):
            energy = energy + jnp.where(me * S + k < live_total, cells[k], 0.0)
        energies.append(energy)

        def from_terms(s):
            rows, cols = tile_of(s)
            return term_stage.at[r, :, rows, cols]

        exchange(from_terms, terms.at[r, pl.ds(me * S, S)], 3 + 2 * r)

        if r == ROUNDS - 1:
            for i, e in enumerate(energies):
                part = jnp.sum(e.reshape(edge // 8, 8, plane), axis=0)
                e_mine[i] = sum(part[:, c * TILE_C : (c + 1) * TILE_C] for c in range(strips))
            exchange(lambda s: e_mine, e_group.at[me], 7)

        arrived(terms.at[r], 3 + 2 * r)
        wide[...] = terms[r].astype(jnp.float32).reshape(slots * TILE_R, TILE_C)
        if r == 0:
            arrived(q_slab, 1)
        for j in range(TILE_R):
            part = wide[pl.ds(j, slots, stride=TILE_R), :].astype(jnp.bfloat16)
            out = dot(choose, part)
            if r == 0:
                summed[pl.ds(j, norb, stride=TILE_R), :] = out
            else:
                summed[pl.ds(j, norb, stride=TILE_R), :] += out
        if r == 0:
            total = summed[...].reshape(norb, TILE_R, TILE_C)
            slab1[...] = (q_slab[...] - damping * total).astype(jnp.bfloat16)
        else:
            final_stage[...] = summed[...].reshape(norb, TILE_R, TILE_C).astype(jnp.bfloat16)

    exchange(lambda s: final_stage.at[pl.ds(s * own, own)], exb.at[:, my_rows, my_cols], 6)

    arrived(e_group, 7)
    e_sum[...] = jnp.sum(e_group[...], axis=0)

    def go_row(d, _):
        pltpu.make_async_remote_copy(
            src_ref=e_sum,
            dst_ref=e_row.at[row],
            send_sem=send_sem.at[8],
            recv_sem=recv_sem.at[8],
            device_id={"row": (row + d) % n_row},
            device_id_type=pl.DeviceIdType.MESH,
        ).start()
        return 0

    lax.fori_loop(1, n_row, go_row, 0)
    pltpu.make_async_copy(e_sum, e_row.at[row], recv_sem.at[8]).start()
    arrived(e_row, 8)
    all_cells = edge * edge * edge * n_row * n_col
    for i in range(ROUNDS):
        energy_out[i] = jnp.sum(jnp.sum(e_row[:, i], axis=0)) / all_cells
    arrived(exb, 6)

    others = n_col - 1
    sent(slab0.at[pl.ds(0, others * own)], 0)
    sent(q_slab.at[pl.ds(0, others * own)], 1)
    for r in range(ROUNDS):
        sent(pack.at[r, pl.ds(0, others * 2 * S)], 2 + 2 * r)
        sent(terms.at[r, pl.ds(0, others * S)], 3 + 2 * r)
    sent(final_stage.at[pl.ds(0, others * own)], 6)
    sent(e_group.at[pl.ds(0, others)], 7)
    if n_row > 1:
        sent(e_row.at[pl.ds(0, n_row - 1)], 8)


def spread_pairs(n_row, n_col, S, orbitals, gradient, offsets, pairs, counts):
    own, edge, plane = orbitals.shape
    norb = own * n_col
    slots = S * n_col
    base = lax.axis_index("row") * norb
    table = jnp.concatenate(
        [
            (pairs - base).reshape(-1),
            counts,
            lax.dynamic_slice_in_dim(offsets, base, norb, 0).reshape(-1),
        ]
    )
    basis, poly = spectral_tables(edge)
    kron = two_parts(np.kron(basis, basis))
    sx = two_parts(np.kron(np.eye(S), basis))
    hbm = pl.BlockSpec(memory_space=pltpu.HBM)
    f32, bf16 = jnp.float32, jnp.bfloat16
    tiles = (norb, TILE_R, TILE_C)
    exchanged, energies = pl.pallas_call(
        functools.partial(spread_kernel, n_row, n_col, S),
        out_shape=(
            jax.ShapeDtypeStruct((own, edge, plane), bf16),
            jax.ShapeDtypeStruct((ROUNDS,), f32),
        ),
        in_specs=[pl.BlockSpec(memory_space=pltpu.SMEM)] + [hbm] * 5,
        out_specs=(pl.BlockSpec(memory_space=pltpu.VMEM), pl.BlockSpec(memory_space=pltpu.SMEM)),
        scratch_shapes=[
            pltpu.VMEM((own, edge, plane), f32),
            pltpu.VMEM((own, edge, plane), f32),
            pltpu.VMEM((2, plane, plane), bf16),
            pltpu.VMEM((2, S * edge, S * edge), bf16),
            pltpu.VMEM((edge, plane), f32),
            pltpu.VMEM((own, edge, plane), bf16),
            pltpu.VMEM((own, edge, plane), f32),
            pltpu.VMEM(tiles, bf16),
            pltpu.VMEM(tiles, f32),
            pltpu.VMEM(tiles, bf16),
            pltpu.VMEM((ROUNDS, slots * 2, TILE_R, TILE_C), bf16),
            pltpu.VMEM((ROUNDS, 2 * S, edge, plane), bf16),
            pltpu.VMEM((S * edge, plane), f32),
            pltpu.VMEM((S * edge, plane), f32),
            pltpu.VMEM((ROUNDS, S, edge, plane), bf16),
            pltpu.VMEM((ROUNDS, slots, TILE_R, TILE_C), bf16),
            pltpu.VMEM((slots * TILE_R, TILE_C), f32),
            pltpu.VMEM((norb * TILE_R, TILE_C), f32),
            pltpu.VMEM(tiles, bf16),
            pltpu.VMEM((ROUNDS, 8, TILE_C), f32),
            pltpu.VMEM((n_col, ROUNDS, 8, TILE_C), f32),
            pltpu.VMEM((ROUNDS, 8, TILE_C), f32),
            pltpu.VMEM((n_row, ROUNDS, 8, TILE_C), f32),
            pltpu.SMEM((slots,), jnp.int32),
            pltpu.SMEM((slots,), jnp.int32),
            pltpu.SemaphoreType.DMA((5,)),
            pltpu.SemaphoreType.DMA((9,)),
            pltpu.SemaphoreType.DMA((9,)),
        ],
        compiler_params=pltpu.CompilerParams(
            collective_id=S, has_side_effects=True, vmem_limit_bytes=60 * 1024 * 1024
        ),
    )(table, orbitals, gradient, jnp.asarray(kron), jnp.asarray(sx), jnp.asarray(poly.astype(np.float32)))
    updated = orbitals - gradient - damping * exchanged.astype(f32)
    return updated, energies


def direct_kernel(
    n_row,
    n_col,
    REMOTE,
    LOCAL,
    pairs,
    counts,
    offsets,
    orb_hbm,
    grad_hbm,
    kron_hbm,
    sx_hbm,
    poly_hbm,
    exchanged,
    energy_out,
    orb,
    grad,
    kron,
    sx,
    poly,
    stage0,
    stage1,
    slab0,
    slab1,
    pack,
    pair_box,
    partner,
    density,
    e_mine,
    e_group,
    e_sum,
    e_row,
    slot_rows,
    slot_of,
    load_sem,
    slot_sem,
    send_sem,
    recv_sem,
):
    me = lax.axis_index("col")
    row = lax.axis_index("row")
    own, edge, plane = orb.shape
    norb = own * n_col
    base = row * norb
    strips = plane // TILE_C
    per_owner = pairs.shape[0]
    mesh_id = pl.DeviceIdType.MESH
    box_stage, slab = (stage0, stage1), (slab0, slab1)

    loads = [
        pltpu.make_async_copy(a, b, load_sem.at[i])
        for i, (a, b) in enumerate(
            ((orb_hbm, orb), (grad_hbm, grad), (kron_hbm, kron), (sx_hbm, sx), (poly_hbm, poly))
        )
    ]
    for one in loads:
        one.start()

    barrier = pltpu.get_barrier_semaphore()
    side, steps = peers(n_col)

    def peer(step):
        return ((me // side + step[0]) % side) * side + (me % side + step[1]) % side

    for step in steps:
        pl.semaphore_signal(barrier, inc=1, device_id={"col": peer(step)}, device_id_type=mesh_id)

    def greet_row(d, _):
        pl.semaphore_signal(barrier, inc=1, device_id={"row": (row + d) % n_row}, device_id_type=mesh_id)
        return 0

    lax.fori_loop(1, n_row, greet_row, 0)

    lane = lax.broadcasted_iota(jnp.int32, (8, TILE_C), 1)

    def place(index, state):
        p, k = index // per_owner, index % per_owner
        at_first = lax.div(pairs[k, 0, p] - base, jnp.int32(own))
        at_second = lax.div(pairs[k, 1, p] - base, jnp.int32(own))
        here = jnp.where(k < counts[p], at_first, -1)
        far = jnp.where(at_first == at_second, -1, here)
        near = jnp.where(at_first == at_second, here, -1)
        out = []
        for device, (count, slots) in zip((far, near), state):
            hit = lane == device
            slots = tuple(jnp.where(hit & (count == s), index, held) for s, held in enumerate(slots))
            out.append((count + hit.astype(jnp.int32), slots))
        return tuple(out)

    none = jnp.full((8, TILE_C), -1, jnp.int32)
    zero = jnp.zeros((8, TILE_C), jnp.int32)
    (far_count, far_slots), (near_count, near_slots) = lax.fori_loop(
        0, n_col * per_owner, place, ((zero, (none,) * REMOTE), (zero, (none,) * LOCAL))
    )
    for s, held in enumerate(far_slots + near_slots):
        slot_rows[pl.ds(s, 1), :] = held[0:1, :]
    over = ((far_count > REMOTE) | (near_count > LOCAL)).astype(jnp.float32)
    overflow = jnp.sum(over[0:1, :], axis=1, keepdims=True)
    to_scalars = pltpu.make_async_copy(slot_rows, slot_of, slot_sem.at[0])
    to_scalars.start()

    def tile_of(s):
        return pl.ds(pl.multiple_of((s // strips) * TILE_R, TILE_R), TILE_R), pl.ds(
            pl.multiple_of((s % strips) * TILE_C, TILE_C), TILE_C
        )

    my_rows, my_cols = tile_of(me)

    def send(src, dst, which, to):
        pltpu.make_async_remote_copy(
            src_ref=src,
            dst_ref=dst,
            send_sem=send_sem.at[which],
            recv_sem=recv_sem.at[which],
            device_id={"col": to},
            device_id_type=mesh_id,
        ).start()

    def arrived(ref, which):
        pltpu.make_async_copy(ref, ref, recv_sem.at[which]).wait()

    def sent(ref, which):
        pltpu.make_async_copy(ref, ref, send_sem.at[which]).wait()

    def send_boxes(r):
        def part(s):
            rows, cols = tile_of(s)
            return box_stage[r].at[:, rows, cols]

        dst = slab[r].at[pl.ds(me * own, own)]
        for step in steps:
            send(part(peer(step)), dst, 2 * r, peer(step))
        pltpu.make_async_copy(part(me), dst, recv_sem.at[2 * r]).start()

    def send_pairs(r):
        dst = pair_box.at[r, :, my_rows, my_cols]

        def fill(to):
            for s in range(REMOTE):
                index = jnp.maximum(slot_of[s, to], 0)
                second = pairs[lax.rem(index, jnp.int32(per_owner)), 1, lax.div(index, jnp.int32(per_owner))]
                pack[r, to, s] = slab[r][jnp.clip(second - base, 0, norb - 1)]

        for step in steps:
            fill(peer(step))
            send(pack.at[r, peer(step)], dst, 2 * r + 1, peer(step))
        fill(me)
        pltpu.make_async_copy(pack.at[r, me], dst, recv_sem.at[2 * r + 1]).start()

    line = lax.broadcasted_iota(jnp.int32, (edge, plane), 0)
    cell = lax.broadcasted_iota(jnp.int32, (edge, plane), 1)

    def work(r, start, number, between=None):
        firsts = []
        for n in range(number):
            code = slot_of[start + n, me]
            index = jnp.maximum(code, 0)
            p = lax.div(index, jnp.int32(per_owner))
            k = lax.rem(index, jnp.int32(per_owner))
            first, second = pairs[k, 0, p], pairs[k, 1, p]
            mine = jnp.clip(first - base - me * own, 0, own - 1)
            firsts.append(jnp.where(code >= 0, mine, -1))
            dx = offsets[0, first] - offsets[0, second]
            dy = offsets[1, first] - offsets[1, second]
            dz = offsets[2, first] - offsets[2, second]
            t = dy * edge + dz
            if start < REMOTE:
                moved = pair_box[r, start + n]
            else:
                moved = box_stage[r][jnp.clip(second - base - me * own, 0, own - 1)]
            moved = moved.astype(jnp.float32)
            moved = pltpu.roll(moved, lax.rem(plane - t, jnp.int32(plane)), 1)
            moved = pltpu.roll(moved, lax.rem(edge - dx, jnp.int32(edge)), 0)
            at_x = line + dx
            at_y = cell // edge + dy
            at_z = cell % edge + dz
            inside = (at_x >= 0) & (at_x < edge) & (at_y >= 0) & (at_y < edge) & (at_z >= 0) & (at_z < edge)
            moved = jnp.where(inside, moved, 0.0)
            partner[pl.ds(n * edge, edge), :] = moved
            density[pl.ds(n * edge, edge), :] = box_stage[r][mine].astype(jnp.float32) * moved
        rows = number * edge

        def along_yz(x):
            high, low = split(x)
            both = dot(jnp.concatenate([high, low], 0), kron[0])
            return both[:rows] + (both[rows:] + dot(high, kron[1]))

        def along_x(x):
            high, low = split(x)
            part = sx[0, pl.ds(0, rows), pl.ds(0, rows)]
            both = dot(jnp.concatenate([part, sx[1, pl.ds(0, rows), pl.ds(0, rows)]], 0), high)
            return both[:rows] + (both[rows:] + dot(part, low))

        modes = along_x(along_yz(density[pl.ds(0, rows), :])).reshape(number, edge, plane)
        scaled = modes * poly[...][None]
        energy = jnp.zeros((8, TILE_C), jnp.float32)
        for n in range(number):
            part = jnp.sum((modes[n] * scaled[n]).reshape(edge // 8, 8, plane), axis=0)
            part = sum(part[:, c * TILE_C : (c + 1) * TILE_C] for c in range(strips))
            energy = energy + jnp.where(firsts[n] >= 0, part, 0.0)
        if between is not None:
            between(energy)
        potential = along_yz(along_x(scaled.reshape(rows, plane)))
        terms = (potential * partner[pl.ds(0, rows), :]).astype(jnp.bfloat16).astype(jnp.float32)
        for o in range(own):
            total = exchanged[o]
            for n in range(number):
                total = total + jnp.where(firsts[n] == o, terms[n * edge : (n + 1) * edge], 0.0)
            exchanged[o] = total
        return energy

    exchanged[...] = jnp.zeros_like(exchanged)
    loads[0].wait()
    box_stage[0][...] = orb[...].astype(jnp.bfloat16)
    pl.semaphore_wait(barrier, n_col - 1 + n_row - 1)
    send_boxes(0)
    to_scalars.wait()
    for one in loads[1:]:
        one.wait()

    def total_of(energy):
        return jnp.sum(jnp.sum(energy, axis=0, keepdims=True), axis=1, keepdims=True)

    half = LOCAL // 2
    kept = []
    for r in range(ROUNDS):
        energy = work(r, REMOTE, half)
        arrived(slab[r], 2 * r)
        send_pairs(r)
        energy = energy + work(r, REMOTE + half, LOCAL - half)
        arrived(pair_box.at[r], 2 * r + 1)
        if r < ROUNDS - 1:
            kept.append(total_of(energy + work(r, 0, REMOTE)))
            box_stage[r + 1][...] = (orb[...] - damping * ((r + 1.0) * grad[...] + exchanged[...])).astype(jnp.bfloat16)
            send_boxes(r + 1)
        else:

            def send_energy(last):
                values = kept + [total_of(energy + last), overflow]
                at = lax.broadcasted_iota(jnp.int32, (1, TILE_C), 1)
                out = jnp.zeros((1, TILE_C), jnp.float32)
                for i, value in enumerate(values):
                    out = jnp.where(at == i, value, out)
                e_mine[...] = out
                for step in steps:
                    send(e_mine, e_group.at[me], 2 * ROUNDS, peer(step))
                pltpu.make_async_copy(e_mine, e_group.at[me], recv_sem.at[2 * ROUNDS]).start()

            work(r, 0, REMOTE, send_energy)

    arrived(e_group, 2 * ROUNDS)
    e_sum[...] = jnp.sum(e_group[...], axis=0)
    last = 2 * ROUNDS + 1

    def go_row(d, _):
        pltpu.make_async_remote_copy(
            src_ref=e_sum,
            dst_ref=e_row.at[row],
            send_sem=send_sem.at[last],
            recv_sem=recv_sem.at[last],
            device_id={"row": (row + d) % n_row},
            device_id_type=mesh_id,
        ).start()
        return 0

    lax.fori_loop(1, n_row, go_row, 0)
    pltpu.make_async_copy(e_sum, e_row.at[row], recv_sem.at[last]).start()
    others = n_col - 1
    for r in range(ROUNDS):
        sent(slab[r].at[pl.ds(0, others * own)], 2 * r)
        sent(pack.at[r, pl.ds(0, others)], 2 * r + 1)
    sent(e_group.at[pl.ds(0, others)], 2 * ROUNDS)
    arrived(e_row, last)
    energy_out[...] = jnp.sum(e_row[...], axis=0) / (edge * edge * edge * n_row * n_col)
    if n_row > 1:
        sent(e_row.at[pl.ds(0, n_row - 1)], last)


def direct_pairs(n_row, n_col, REMOTE, LOCAL, orbitals, gradient, offsets, pairs, counts):
    own, edge, plane = orbitals.shape
    norb = own * n_col
    basis, poly = spectral_tables(edge)
    kron = two_parts(np.kron(basis, basis))
    most = max(REMOTE, LOCAL - LOCAL // 2)
    sx = two_parts(np.kron(np.eye(most), basis))
    hbm = pl.BlockSpec(memory_space=pltpu.HBM)
    smem = pl.BlockSpec(memory_space=pltpu.SMEM)
    vmem = pl.BlockSpec(memory_space=pltpu.VMEM)
    f32, bf16 = jnp.float32, jnp.bfloat16
    return pl.pallas_call(
        functools.partial(direct_kernel, n_row, n_col, REMOTE, LOCAL),
        out_shape=(
            jax.ShapeDtypeStruct((own, edge, plane), f32),
            jax.ShapeDtypeStruct((1, TILE_C), f32),
        ),
        in_specs=[smem] * 3 + [hbm] * 5,
        out_specs=(vmem, vmem),
        scratch_shapes=[
            pltpu.VMEM((own, edge, plane), f32),
            pltpu.VMEM((own, edge, plane), f32),
            pltpu.VMEM((2, plane, plane), bf16),
            pltpu.VMEM((2, most * edge, most * edge), bf16),
            pltpu.VMEM((edge, plane), f32),
            pltpu.VMEM((own, edge, plane), bf16),
            pltpu.VMEM((own, edge, plane), bf16),
            pltpu.VMEM((norb, TILE_R, TILE_C), bf16),
            pltpu.VMEM((norb, TILE_R, TILE_C), bf16),
            pltpu.VMEM((ROUNDS, n_col, REMOTE, TILE_R, TILE_C), bf16),
            pltpu.VMEM((ROUNDS, REMOTE, edge, plane), bf16),
            pltpu.VMEM((most * edge, plane), f32),
            pltpu.VMEM((most * edge, plane), f32),
            pltpu.VMEM((1, TILE_C), f32),
            pltpu.VMEM((n_col, 1, TILE_C), f32),
            pltpu.VMEM((1, TILE_C), f32),
            pltpu.VMEM((n_row, 1, TILE_C), f32),
            pltpu.VMEM((16, TILE_C), jnp.int32),
            pltpu.SMEM((16, TILE_C), jnp.int32),
            pltpu.SemaphoreType.DMA((5,)),
            pltpu.SemaphoreType.DMA((1,)),
            pltpu.SemaphoreType.DMA((2 * ROUNDS + 2,)),
            pltpu.SemaphoreType.DMA((2 * ROUNDS + 2,)),
        ],
        compiler_params=pltpu.CompilerParams(
            collective_id=1, has_side_effects=True, vmem_limit_bytes=60 * 1024 * 1024
        ),
    )(
        pairs.transpose(1, 2, 0),
        counts,
        offsets.T,
        orbitals,
        gradient,
        jnp.asarray(kron),
        jnp.asarray(sx),
        jnp.asarray(poly.astype(np.float32)),
    )


def local(n_row, n_col, REMOTE, LOCAL, S, orbitals, gradient, offsets, pairs, counts):
    exchanged, values = direct_pairs(n_row, n_col, REMOTE, LOCAL, orbitals, gradient, offsets, pairs, counts)

    def enough():
        return orbitals - gradient - damping * exchanged, values[0, :ROUNDS]

    def general():
        return spread_pairs(n_row, n_col, S, orbitals, gradient, offsets, pairs, counts)

    return lax.cond(values[0, ROUNDS] > 0, general, enough)


def solution(mesh):
    n_row, n_col = mesh.shape["row"], mesh.shape["col"]
    both = P(("row", "col"), None, None)
    return jax.shard_map(
        functools.partial(local, n_row, n_col, 5, 6, 4),
        mesh=mesh,
        in_specs=(both, both, P(), P("row", None, None), P("row")),
        out_specs=(both, P()),
        check_vma=False,
    )
```

```python
import functools

import jax
import jax.numpy as jnp
import ml_dtypes
import numpy as np
from jax import lax
from jax.experimental import pallas as pl
from jax.experimental.pallas import tpu as pltpu
from jax.sharding import PartitionSpec as P

SWEEPS = 12
ROUNDS = 2
TILE_R = 16
TILE_C = 128
screen_mu = 0.1
damping = 0.5


def spectral_tables(edge):
    k = np.arange(1, edge + 1)
    basis = np.sqrt(2.0 / (edge + 1)) * np.sin(np.pi * np.outer(k, k) / (edge + 1))
    line = 2.0 * np.cos(np.pi * k / (edge + 1))
    eig = (6.0 + screen_mu) - (line[:, None, None] + line[None, :, None] + line[None, None, :])
    c, h = 6.0 + screen_mu, 6.0
    g = c / h
    q = 1.0 / g
    u = np.zeros_like(eig)
    t = np.ones_like(eig)
    d = t / c
    for _ in range(SWEEPS):
        u = u + d
        t = t - eig * d
        q_new = 1.0 / (2.0 * g - q)
        d = q_new * q * d + (2.0 * q_new / h) * t
        q = q_new
    return basis, u.reshape(edge, edge * edge)


def two_parts(x):
    high = x.astype(ml_dtypes.bfloat16)
    return np.stack([high, (x - high.astype(np.float64)).astype(ml_dtypes.bfloat16)])


def split(x):
    high = x.astype(jnp.bfloat16)
    return high, (x - high.astype(jnp.float32)).astype(jnp.bfloat16)


def dot(a, b):
    return jnp.dot(a, b, preferred_element_type=jnp.float32)


def dot_split(a, b):
    (a_high, a_low), (b_high, b_low) = a, b
    return dot(a_high, b_high) + (dot(a_low, b_high) + dot(a_high, b_low))


def peers(n_col):
    side = int(round(n_col**0.5))
    steps = [(a, b) for a in range(side) for b in range(side) if a + b > 0]
    return side, sorted(steps, key=lambda p: -(min(p[0], side - p[0]) + min(p[1], side - p[1])))


def spread_kernel(
    n_row,
    n_col,
    S,
    tbl,
    orb_hbm,
    grad_hbm,
    kron_hbm,
    sx_hbm,
    poly_hbm,
    exb,
    energy_out,
    orb,
    grad,
    kron,
    sx,
    poly,
    box_stage,
    q_stage,
    slab0,
    q_slab,
    slab1,
    pack,
    pair_box,
    partner,
    density,
    term_stage,
    terms,
    wide,
    summed,
    final_stage,
    e_mine,
    e_group,
    e_sum,
    e_row,
    first_of,
    second_of,
    load_sem,
    send_sem,
    recv_sem,
):
    me = lax.axis_index("col")
    row = lax.axis_index("row")
    own, edge, plane = orb.shape
    norb = own * n_col
    slots = S * n_col
    halves = edge // TILE_R
    strips = plane // TILE_C

    loads = [
        pltpu.make_async_copy(a, b, load_sem.at[i])
        for i, (a, b) in enumerate(
            ((orb_hbm, orb), (grad_hbm, grad), (kron_hbm, kron), (sx_hbm, sx), (poly_hbm, poly))
        )
    ]
    for one in loads:
        one.start()

    barrier = pltpu.get_barrier_semaphore()

    def greet_col(d, _):
        pl.semaphore_signal(barrier, inc=1, device_id={"col": (me + d) % n_col}, device_id_type=pl.DeviceIdType.MESH)
        return 0

    def greet_row(d, _):
        pl.semaphore_signal(barrier, inc=1, device_id={"row": (row + d) % n_row}, device_id_type=pl.DeviceIdType.MESH)
        return 0

    lax.fori_loop(1, n_col, greet_col, 0)
    lax.fori_loop(1, n_row, greet_row, 0)

    count_at = n_col * 8
    offset_at = count_at + n_col

    def rank(r, firsts):
        def seek(p, state):
            start, found = state
            count = tbl[count_at + p]
            inside = (r >= start) & (r < start + count)
            return start + count, jnp.where(inside, p * 4 + r - start, found)

        total, found = lax.fori_loop(0, n_col, seek, (jnp.int32(0), jnp.int32(-1)))
        at = jnp.maximum(found, 0) * 2
        first = tbl[at]
        first_of[r] = first
        second_of[r] = tbl[at + 1]
        lane = lax.broadcasted_iota(jnp.int32, (norb, slots), 1)
        return jnp.where(lane == r, jnp.where(found >= 0, first, -1), firsts)

    firsts = lax.fori_loop(0, slots, rank, jnp.full((norb, slots), -1, jnp.int32))
    choose = (lax.broadcasted_iota(jnp.int32, (norb, slots), 0) == firsts).astype(jnp.float32).astype(jnp.bfloat16)

    def total_live(p, acc):
        return acc + tbl[count_at + p]

    live_total = lax.fori_loop(0, n_col, total_live, jnp.int32(0))

    def tile_of(s):
        return pl.ds(pl.multiple_of((s // strips) * TILE_R, TILE_R), TILE_R), pl.ds(
            pl.multiple_of((s % strips) * TILE_C, TILE_C), TILE_C
        )

    my_rows, my_cols = tile_of(me)

    def exchange(src_of, dst, which, before=None):
        side, steps = peers(n_col)
        for dy, dz in steps:
            to = ((me // side + dy) % side) * side + (me % side + dz) % side
            if before is not None:
                before(to)
            pltpu.make_async_remote_copy(
                src_ref=src_of(to),
                dst_ref=dst,
                send_sem=send_sem.at[which],
                recv_sem=recv_sem.at[which],
                device_id={"col": to},
                device_id_type=pl.DeviceIdType.MESH,
            ).start()
        if before is not None:
            before(me)
        pltpu.make_async_copy(src_of(me), dst, recv_sem.at[which]).start()

    def arrived(ref, which):
        pltpu.make_async_copy(ref, ref, recv_sem.at[which]).wait()

    def sent(ref, which):
        pltpu.make_async_copy(ref, ref, send_sem.at[which]).wait()

    loads[0].wait()
    box_stage[...] = orb[...].astype(jnp.bfloat16)
    pl.semaphore_wait(barrier, n_col - 1 + n_row - 1)

    def from_boxes(s):
        rows, cols = tile_of(s)
        return box_stage.at[:, rows, cols]

    def from_q(s):
        rows, cols = tile_of(s)
        return q_stage.at[:, rows, cols]

    mine4 = pl.ds(me * own, own)
    exchange(from_boxes, slab0.at[mine4], 0)
    loads[1].wait()
    q_stage[...] = orb[...] - damping * grad[...]
    exchange(from_q, q_slab.at[mine4], 1)
    for one in loads[2:]:
        one.wait()

    energies = []
    for r in range(ROUNDS):
        slab = (slab0, slab1)[r]
        if r == 0:
            arrived(slab0, 0)

        def fill(p):
            for k in range(S):
                pack[r, p * 2 * S + 2 * k] = slab[first_of[p * S + k]]
                pack[r, p * 2 * S + 2 * k + 1] = slab[second_of[p * S + k]]

        def from_pack(p):
            return pack.at[r, pl.ds(p * 2 * S, 2 * S)]

        exchange(from_pack, pair_box.at[r, :, my_rows, my_cols], 2 + 2 * r, fill)
        arrived(pair_box.at[r], 2 + 2 * r)

        lane = lax.broadcasted_iota(jnp.int32, (edge, plane), 1)
        line = lax.broadcasted_iota(jnp.int32, (edge, plane), 0)
        for k in range(S):
            a = offset_at + 3 * first_of[me * S + k]
            b = offset_at + 3 * second_of[me * S + k]
            dx = tbl[a] - tbl[b]
            dy = tbl[a + 1] - tbl[b + 1]
            dz = tbl[a + 2] - tbl[b + 2]
            t = dy * edge + dz
            moved = pair_box[r, 2 * k + 1].astype(jnp.float32)
            moved = pltpu.roll(moved, lax.rem(plane - t, jnp.int32(plane)), 1)
            moved = pltpu.roll(moved, lax.rem(edge - dx, jnp.int32(edge)), 0)
            at_x = line + dx
            at_y = lane // edge + dy
            at_z = lane % edge + dz
            inside = (
                (at_x >= 0) & (at_x < edge) & (at_y >= 0) & (at_y < edge) & (at_z >= 0) & (at_z < edge)
            )
            moved = jnp.where(inside, moved, 0.0)
            partner[pl.ds(k * edge, edge), :] = moved
            density[pl.ds(k * edge, edge), :] = pair_box[r, 2 * k].astype(jnp.float32) * moved

        yz = kron[0], kron[1]
        along_x = sx[0], sx[1]
        modes = dot_split(split(density[...]), yz)
        modes = dot_split(along_x, split(modes)).reshape(S, edge, plane) * poly[...][None]
        modes = dot_split(along_x, split(modes.reshape(S * edge, plane)))
        potential = dot_split(split(modes), yz)
        term_stage[r] = (potential * partner[...]).astype(jnp.bfloat16).reshape(S, edge, plane)
        cells = (density[...] * potential).reshape(S, edge, plane)
        energy = jnp.zeros((edge, plane), jnp.float32)
        for k in range(S):
            energy = energy + jnp.where(me * S + k < live_total, cells[k], 0.0)
        energies.append(energy)

        def from_terms(s):
            rows, cols = tile_of(s)
            return term_stage.at[r, :, rows, cols]

        exchange(from_terms, terms.at[r, pl.ds(me * S, S)], 3 + 2 * r)

        if r == ROUNDS - 1:
            for i, e in enumerate(energies):
                part = jnp.sum(e.reshape(edge // 8, 8, plane), axis=0)
                e_mine[i] = sum(part[:, c * TILE_C : (c + 1) * TILE_C] for c in range(strips))
            exchange(lambda s: e_mine, e_group.at[me], 7)

        arrived(terms.at[r], 3 + 2 * r)
        wide[...] = terms[r].astype(jnp.float32).reshape(slots * TILE_R, TILE_C)
        if r == 0:
            arrived(q_slab, 1)
        for j in range(TILE_R):
            part = wide[pl.ds(j, slots, stride=TILE_R), :].astype(jnp.bfloat16)
            out = dot(choose, part)
            if r == 0:
                summed[pl.ds(j, norb, stride=TILE_R), :] = out
            else:
                summed[pl.ds(j, norb, stride=TILE_R), :] += out
        if r == 0:
            total = summed[...].reshape(norb, TILE_R, TILE_C)
            slab1[...] = (q_slab[...] - damping * total).astype(jnp.bfloat16)
        else:
            final_stage[...] = summed[...].reshape(norb, TILE_R, TILE_C).astype(jnp.bfloat16)

    exchange(lambda s: final_stage.at[pl.ds(s * own, own)], exb.at[:, my_rows, my_cols], 6)

    arrived(e_group, 7)
    e_sum[...] = jnp.sum(e_group[...], axis=0)

    def go_row(d, _):
        pltpu.make_async_remote_copy(
            src_ref=e_sum,
            dst_ref=e_row.at[row],
            send_sem=send_sem.at[8],
            recv_sem=recv_sem.at[8],
            device_id={"row": (row + d) % n_row},
            device_id_type=pl.DeviceIdType.MESH,
        ).start()
        return 0

    lax.fori_loop(1, n_row, go_row, 0)
    pltpu.make_async_copy(e_sum, e_row.at[row], recv_sem.at[8]).start()
    arrived(e_row, 8)
    all_cells = edge * edge * edge * n_row * n_col
    for i in range(ROUNDS):
        energy_out[i] = jnp.sum(jnp.sum(e_row[:, i], axis=0)) / all_cells
    arrived(exb, 6)

    others = n_col - 1
    sent(slab0.at[pl.ds(0, others * own)], 0)
    sent(q_slab.at[pl.ds(0, others * own)], 1)
    for r in range(ROUNDS):
        sent(pack.at[r, pl.ds(0, others * 2 * S)], 2 + 2 * r)
        sent(terms.at[r, pl.ds(0, others * S)], 3 + 2 * r)
    sent(final_stage.at[pl.ds(0, others * own)], 6)
    sent(e_group.at[pl.ds(0, others)], 7)
    if n_row > 1:
        sent(e_row.at[pl.ds(0, n_row - 1)], 8)


def spread_pairs(n_row, n_col, S, orbitals, gradient, offsets, pairs, counts):
    own, edge, plane = orbitals.shape
    norb = own * n_col
    slots = S * n_col
    base = lax.axis_index("row") * norb
    table = jnp.concatenate(
        [
            (pairs - base).reshape(-1),
            counts,
            lax.dynamic_slice_in_dim(offsets, base, norb, 0).reshape(-1),
        ]
    )
    basis, poly = spectral_tables(edge)
    kron = two_parts(np.kron(basis, basis))
    sx = two_parts(np.kron(np.eye(S), basis))
    hbm = pl.BlockSpec(memory_space=pltpu.HBM)
    f32, bf16 = jnp.float32, jnp.bfloat16
    tiles = (norb, TILE_R, TILE_C)
    exchanged, energies = pl.pallas_call(
        functools.partial(spread_kernel, n_row, n_col, S),
        out_shape=(
            jax.ShapeDtypeStruct((own, edge, plane), bf16),
            jax.ShapeDtypeStruct((ROUNDS,), f32),
        ),
        in_specs=[pl.BlockSpec(memory_space=pltpu.SMEM)] + [hbm] * 5,
        out_specs=(pl.BlockSpec(memory_space=pltpu.VMEM), pl.BlockSpec(memory_space=pltpu.SMEM)),
        scratch_shapes=[
            pltpu.VMEM((own, edge, plane), f32),
            pltpu.VMEM((own, edge, plane), f32),
            pltpu.VMEM((2, plane, plane), bf16),
            pltpu.VMEM((2, S * edge, S * edge), bf16),
            pltpu.VMEM((edge, plane), f32),
            pltpu.VMEM((own, edge, plane), bf16),
            pltpu.VMEM((own, edge, plane), f32),
            pltpu.VMEM(tiles, bf16),
            pltpu.VMEM(tiles, f32),
            pltpu.VMEM(tiles, bf16),
            pltpu.VMEM((ROUNDS, slots * 2, TILE_R, TILE_C), bf16),
            pltpu.VMEM((ROUNDS, 2 * S, edge, plane), bf16),
            pltpu.VMEM((S * edge, plane), f32),
            pltpu.VMEM((S * edge, plane), f32),
            pltpu.VMEM((ROUNDS, S, edge, plane), bf16),
            pltpu.VMEM((ROUNDS, slots, TILE_R, TILE_C), bf16),
            pltpu.VMEM((slots * TILE_R, TILE_C), f32),
            pltpu.VMEM((norb * TILE_R, TILE_C), f32),
            pltpu.VMEM(tiles, bf16),
            pltpu.VMEM((ROUNDS, 8, TILE_C), f32),
            pltpu.VMEM((n_col, ROUNDS, 8, TILE_C), f32),
            pltpu.VMEM((ROUNDS, 8, TILE_C), f32),
            pltpu.VMEM((n_row, ROUNDS, 8, TILE_C), f32),
            pltpu.SMEM((slots,), jnp.int32),
            pltpu.SMEM((slots,), jnp.int32),
            pltpu.SemaphoreType.DMA((5,)),
            pltpu.SemaphoreType.DMA((9,)),
            pltpu.SemaphoreType.DMA((9,)),
        ],
        compiler_params=pltpu.CompilerParams(
            collective_id=S, has_side_effects=True, vmem_limit_bytes=60 * 1024 * 1024
        ),
    )(table, orbitals, gradient, jnp.asarray(kron), jnp.asarray(sx), jnp.asarray(poly.astype(np.float32)))
    updated = orbitals - gradient - damping * exchanged.astype(f32)
    return updated, energies


def flipped(x, edge):
    per_tile = TILE_C // edge
    tiles = x.shape[1] // TILE_C
    block = lax.broadcasted_iota(jnp.int32, (1, TILE_C), 1) // edge
    out = []
    for t in reversed(range(tiles)):
        tile = x[:, t * TILE_C : (t + 1) * TILE_C]
        step = per_tile // 2
        while step:
            back = pltpu.roll(tile, TILE_C - step * edge, 1)
            if 2 * step == per_tile:
                tile = back
            else:
                ahead = pltpu.roll(tile, step * edge, 1)
                tile = jnp.where(block // step % 2 == 0, back, ahead)
            step //= 2
        out.append(tile)
    return jnp.concatenate(out, 1)


def folded(basis, poly):
    edge = basis.shape[0]
    half = [np.kron(basis[i::2, : edge // 2].T, basis) for i in range(2)]
    kron = np.stack([two_parts(x) for x in half + [x.T for x in half]])
    poly = poly.reshape(edge, edge, edge)
    poly = np.concatenate([poly[:, 0::2], poly[:, 1::2]], 1)
    return kron, poly.reshape(edge, edge * edge)


def direct_kernel(
    n_row,
    n_col,
    REMOTE,
    LOCAL,
    pairs_hbm,
    counts_hbm,
    offsets_hbm,
    orb_hbm,
    grad_hbm,
    kron_hbm,
    sx_hbm,
    poly_hbm,
    exchanged,
    energy_out,
    over_out,
    pairs,
    counts,
    offsets,
    orb,
    grad,
    kron,
    sx,
    poly,
    stage0,
    stage1,
    slab0,
    slab1,
    pack,
    pair_box,
    partner,
    density,
    e_mine,
    e_group,
    e_sum,
    e_row,
    slot_rows,
    slot_of,
    load_sem,
    slot_sem,
    send_sem,
    recv_sem,
):
    me = lax.axis_index("col")
    row = lax.axis_index("row")
    own, edge, plane = orb.shape
    norb = own * n_col
    base = row * norb
    strips = plane // TILE_C
    per_owner = pairs.shape[0]
    mesh_id = pl.DeviceIdType.MESH
    box_stage, slab = (stage0, stage1), (slab0, slab1)

    barrier = pltpu.get_barrier_semaphore()
    side, steps = peers(n_col)

    def peer(step):
        return ((me // side + step[0]) % side) * side + (me % side + step[1]) % side

    for step in steps:
        pl.semaphore_signal(barrier, inc=1, device_id={"col": peer(step)}, device_id_type=mesh_id)

    def greet_row(d, _):
        pl.semaphore_signal(barrier, inc=1, device_id={"row": (row + d) % n_row}, device_id_type=mesh_id)
        return 0

    lax.fori_loop(1, n_row, greet_row, 0)

    sources = (pairs_hbm, counts_hbm, offsets_hbm, orb_hbm, grad_hbm, kron_hbm, sx_hbm, poly_hbm)
    loads = [
        pltpu.make_async_copy(a, b, load_sem.at[i])
        for i, (a, b) in enumerate(zip(sources, (pairs, counts, offsets, orb, grad, kron, sx, poly)))
    ]
    for one in loads[:4]:
        one.start()
    for one in loads[:3]:
        one.wait()

    lane = lax.broadcasted_iota(jnp.int32, (8, TILE_C), 1)

    def place(index, state):
        p, k = index // per_owner, index % per_owner
        at_first = lax.div(pairs[k, 0, p] - base, jnp.int32(own))
        at_second = lax.div(pairs[k, 1, p] - base, jnp.int32(own))
        here = jnp.where(k < counts[p], at_first, -1)
        far = jnp.where(at_first == at_second, -1, here)
        near = jnp.where(at_first == at_second, here, -1)
        out = []
        for device, (count, slots) in zip((far, near), state):
            hit = lane == device
            slots = tuple(jnp.where(hit & (count == s), index, held) for s, held in enumerate(slots))
            out.append((count + hit.astype(jnp.int32), slots))
        return tuple(out)

    none = jnp.full((8, TILE_C), -1, jnp.int32)
    zero = jnp.zeros((8, TILE_C), jnp.int32)
    (far_count, far_slots), (near_count, near_slots) = lax.fori_loop(
        0, n_col * per_owner, place, ((zero, (none,) * REMOTE), (zero, (none,) * LOCAL))
    )
    for s, held in enumerate(far_slots + near_slots):
        slot_rows[pl.ds(s, 1), :] = held[0:1, :]
    over = ((far_count > REMOTE) | (near_count > LOCAL)).astype(jnp.float32)
    overflow = jnp.sum(over[0:1, :], axis=1, keepdims=True)
    to_scalars = pltpu.make_async_copy(slot_rows, slot_of, slot_sem.at[0])
    to_scalars.start()

    def tile_of(s):
        return pl.ds(pl.multiple_of((s // strips) * TILE_R, TILE_R), TILE_R), pl.ds(
            pl.multiple_of((s % strips) * TILE_C, TILE_C), TILE_C
        )

    my_rows, my_cols = tile_of(me)

    def send(src, dst, which, to):
        pltpu.make_async_remote_copy(
            src_ref=src,
            dst_ref=dst,
            send_sem=send_sem.at[which],
            recv_sem=recv_sem.at[which],
            device_id={"col": to},
            device_id_type=mesh_id,
        ).start()

    def arrived(ref, which):
        pltpu.make_async_copy(ref, ref, recv_sem.at[which]).wait()

    def sent(ref, which):
        pltpu.make_async_copy(ref, ref, send_sem.at[which]).wait()

    def send_boxes(r):
        def part(s):
            rows, cols = tile_of(s)
            return box_stage[r].at[:, rows, cols]

        dst = slab[r].at[pl.ds(me * own, own)]
        for step in steps:
            send(part(peer(step)), dst, 2 * r, peer(step))
        pltpu.make_async_copy(part(me), dst, recv_sem.at[2 * r]).start()

    def send_pairs(r):
        dst = pair_box.at[r, :, my_rows, my_cols]

        def fill(to):
            for s in range(REMOTE):
                index = jnp.maximum(slot_of[s, to], 0)
                second = pairs[lax.rem(index, jnp.int32(per_owner)), 1, lax.div(index, jnp.int32(per_owner))]
                pack[r, to, s] = slab[r][jnp.clip(second - base, 0, norb - 1)]

        for step in steps:
            fill(peer(step))
            send(pack.at[r, peer(step)], dst, 2 * r + 1, peer(step))
        fill(me)
        pltpu.make_async_copy(pack.at[r, me], dst, recv_sem.at[2 * r + 1]).start()

    line = lax.broadcasted_iota(jnp.int32, (edge, 1), 0)
    cell = lax.broadcasted_iota(jnp.int32, (1, plane), 1)

    def work(r, start, number, between=None):
        firsts = []
        for n in range(number):
            code = slot_of[start + n, me]
            index = jnp.maximum(code, 0)
            p = lax.div(index, jnp.int32(per_owner))
            k = lax.rem(index, jnp.int32(per_owner))
            first, second = pairs[k, 0, p], pairs[k, 1, p]
            mine = jnp.clip(first - base - me * own, 0, own - 1)
            firsts.append(jnp.where(code >= 0, mine, -1))
            dx = offsets[0, first] - offsets[0, second]
            dy = offsets[1, first] - offsets[1, second]
            dz = offsets[2, first] - offsets[2, second]
            t = dy * edge + dz
            if start < REMOTE:
                moved = pair_box[r, start + n]
            else:
                moved = box_stage[r][jnp.clip(second - base - me * own, 0, own - 1)]
            moved = moved.astype(jnp.float32)
            moved = pltpu.roll(moved, lax.rem(plane - t, jnp.int32(plane)), 1)
            moved = pltpu.roll(moved, lax.rem(edge - dx, jnp.int32(edge)), 0)
            at_x = line + dx
            at_y = cell // edge + dy
            at_z = cell % edge + dz
            inside_x = ((at_x >= 0) & (at_x < edge)).astype(jnp.float32)
            inside_yz = ((at_y >= 0) & (at_y < edge) & (at_z >= 0) & (at_z < edge)).astype(jnp.float32)
            moved = moved * inside_yz * inside_x
            partner[pl.ds(n * edge, edge), :] = moved
            density[pl.ds(n * edge, edge), :] = box_stage[r][mine].astype(jnp.float32) * moved
        rows = number * edge

        def halves(x, which):
            high, low = split(x)
            both = dot(jnp.concatenate([high, low], 0), kron[which, 0])
            return both[:rows] + (both[rows:] + dot(high, kron[which, 1]))

        def to_modes(x):
            near, far = x[:, : plane // 2], flipped(x[:, plane // 2 :], edge)
            return jnp.concatenate([halves(near + far, 0), halves(near - far, 1)], 1)

        def to_cells(x):
            even, odd = halves(x[:, : plane // 2], 2), halves(x[:, plane // 2 :], 3)
            return jnp.concatenate([even + odd, flipped(even - odd, edge)], 1)

        def along_x(x):
            high, low = split(x)
            part = sx[0, pl.ds(0, rows), pl.ds(0, rows)]
            both = dot(jnp.concatenate([part, sx[1, pl.ds(0, rows), pl.ds(0, rows)]], 0), high)
            return both[:rows] + (both[rows:] + dot(part, low))

        modes = along_x(to_modes(density[pl.ds(0, rows), :])).reshape(number, edge, plane)
        scaled = modes * poly[...][None]
        energy = jnp.zeros((8, TILE_C), jnp.float32)
        for n in range(number):
            part = jnp.sum((modes[n] * scaled[n]).reshape(edge // 8, 8, plane), axis=0)
            part = sum(part[:, c * TILE_C : (c + 1) * TILE_C] for c in range(strips))
            energy = energy + jnp.where(firsts[n] >= 0, part, 0.0)
        if between is not None:
            between(energy)
        potential = to_cells(along_x(scaled.reshape(rows, plane)))
        terms = (potential * partner[pl.ds(0, rows), :]).astype(jnp.bfloat16).astype(jnp.float32)
        for o in range(own):
            total = exchanged[o]
            for n in range(number):
                total = total + jnp.where(firsts[n] == o, terms[n * edge : (n + 1) * edge], 0.0)
            exchanged[o] = total
        return energy

    exchanged[...] = jnp.zeros_like(exchanged)
    loads[3].wait()
    for one in loads[4:]:
        one.start()
    box_stage[0][...] = orb[...].astype(jnp.bfloat16)
    pl.semaphore_wait(barrier, n_col - 1 + n_row - 1)
    send_boxes(0)
    to_scalars.wait()
    for one in loads[4:]:
        one.wait()

    def total_of(energy):
        return jnp.sum(jnp.sum(energy, axis=0, keepdims=True), axis=1, keepdims=True)

    half = LOCAL // 2
    kept = []
    for r in range(ROUNDS):
        energy = work(r, REMOTE, half)
        arrived(slab[r], 2 * r)
        send_pairs(r)
        energy = energy + work(r, REMOTE + half, LOCAL - half)
        arrived(pair_box.at[r], 2 * r + 1)
        if r < ROUNDS - 1:
            kept.append(total_of(energy + work(r, 0, REMOTE)))
            box_stage[r + 1][...] = (orb[...] - damping * ((r + 1.0) * grad[...] + exchanged[...])).astype(jnp.bfloat16)
            send_boxes(r + 1)
        else:

            def send_energy(last):
                values = kept + [total_of(energy + last), overflow]
                at = lax.broadcasted_iota(jnp.int32, (1, TILE_C), 1)
                out = jnp.zeros((1, TILE_C), jnp.float32)
                for i, value in enumerate(values):
                    out = jnp.where(at == i, value, out)
                e_mine[...] = out
                for step in steps:
                    send(e_mine, e_group.at[me], 2 * ROUNDS, peer(step))
                pltpu.make_async_copy(e_mine, e_group.at[me], recv_sem.at[2 * ROUNDS]).start()

            work(r, 0, REMOTE, send_energy)

    arrived(e_group, 2 * ROUNDS)
    e_sum[...] = jnp.sum(e_group[...], axis=0)
    last = 2 * ROUNDS + 1

    def go_row(d, _):
        pltpu.make_async_remote_copy(
            src_ref=e_sum,
            dst_ref=e_row.at[row],
            send_sem=send_sem.at[last],
            recv_sem=recv_sem.at[last],
            device_id={"row": (row + d) % n_row},
            device_id_type=mesh_id,
        ).start()
        return 0

    lax.fori_loop(1, n_row, go_row, 0)
    pltpu.make_async_copy(e_sum, e_row.at[row], recv_sem.at[last]).start()
    others = n_col - 1
    for r in range(ROUNDS):
        sent(slab[r].at[pl.ds(0, others * own)], 2 * r)
        sent(pack.at[r, pl.ds(0, others)], 2 * r + 1)
    sent(e_group.at[pl.ds(0, others)], 2 * ROUNDS)
    arrived(e_row, last)
    values = jnp.sum(e_row[...], axis=0)
    at = lax.broadcasted_iota(jnp.int32, (1, TILE_C), 1)
    for i in range(ROUNDS):
        energy_out[i] = jnp.sum(jnp.where(at == i, values, 0.0)) / (edge * edge * edge * n_row * n_col)
    over_out[0] = jnp.sum(jnp.where(at == ROUNDS, values, 0.0))
    if n_row > 1:
        sent(e_row.at[pl.ds(0, n_row - 1)], last)


def direct_pairs(n_row, n_col, REMOTE, LOCAL, orbitals, gradient, offsets, pairs, counts):
    own, edge, plane = orbitals.shape
    norb = own * n_col
    basis, poly = spectral_tables(edge)
    kron, poly = folded(basis, poly)
    most = max(REMOTE, LOCAL - LOCAL // 2)
    sx = two_parts(np.kron(np.eye(most), basis))
    smem = pl.BlockSpec(memory_space=pltpu.SMEM)
    vmem = pl.BlockSpec(memory_space=pltpu.VMEM)
    f32, bf16 = jnp.float32, jnp.bfloat16
    return pl.pallas_call(
        functools.partial(direct_kernel, n_row, n_col, REMOTE, LOCAL),
        out_shape=(
            jax.ShapeDtypeStruct((own, edge, plane), f32),
            jax.ShapeDtypeStruct((ROUNDS,), f32),
            jax.ShapeDtypeStruct((1,), f32),
        ),
        in_specs=[pl.BlockSpec(memory_space=pl.ANY)] * 8,
        out_specs=(vmem, smem, smem),
        scratch_shapes=[
            pltpu.SMEM((pairs.shape[1], 2, n_col), jnp.int32),
            pltpu.SMEM((n_col,), jnp.int32),
            pltpu.SMEM((3, offsets.shape[0]), jnp.int32),
            pltpu.VMEM((own, edge, plane), f32),
            pltpu.VMEM((own, edge, plane), f32),
            pltpu.VMEM((4, 2, plane // 2, plane // 2), bf16),
            pltpu.VMEM((2, most * edge, most * edge), bf16),
            pltpu.VMEM((edge, plane), f32),
            pltpu.VMEM((own, edge, plane), bf16),
            pltpu.VMEM((own, edge, plane), bf16),
            pltpu.VMEM((norb, TILE_R, TILE_C), bf16),
            pltpu.VMEM((norb, TILE_R, TILE_C), bf16),
            pltpu.VMEM((ROUNDS, n_col, REMOTE, TILE_R, TILE_C), bf16),
            pltpu.VMEM((ROUNDS, REMOTE, edge, plane), bf16),
            pltpu.VMEM((most * edge, plane), f32),
            pltpu.VMEM((most * edge, plane), f32),
            pltpu.VMEM((1, TILE_C), f32),
            pltpu.VMEM((n_col, 1, TILE_C), f32),
            pltpu.VMEM((1, TILE_C), f32),
            pltpu.VMEM((n_row, 1, TILE_C), f32),
            pltpu.VMEM((16, TILE_C), jnp.int32),
            pltpu.SMEM((16, TILE_C), jnp.int32),
            pltpu.SemaphoreType.DMA((8,)),
            pltpu.SemaphoreType.DMA((1,)),
            pltpu.SemaphoreType.DMA((2 * ROUNDS + 2,)),
            pltpu.SemaphoreType.DMA((2 * ROUNDS + 2,)),
        ],
        compiler_params=pltpu.CompilerParams(
            collective_id=1, has_side_effects=True, vmem_limit_bytes=60 * 1024 * 1024
        ),
    )(
        pairs.transpose(1, 2, 0),
        counts,
        offsets.T,
        orbitals,
        gradient,
        jnp.asarray(kron),
        jnp.asarray(sx),
        jnp.asarray(poly.astype(np.float32)),
    )


def local(n_row, n_col, REMOTE, LOCAL, S, orbitals, gradient, offsets, pairs, counts):
    exchanged, energies, over = direct_pairs(n_row, n_col, REMOTE, LOCAL, orbitals, gradient, offsets, pairs, counts)

    def enough():
        return orbitals - gradient - damping * exchanged, energies

    def general():
        return spread_pairs(n_row, n_col, S, orbitals, gradient, offsets, pairs, counts)

    return lax.cond(over[0] > 0, general, enough)


def solution(mesh):
    n_row, n_col = mesh.shape["row"], mesh.shape["col"]
    both = P(("row", "col"), None, None)
    return jax.shard_map(
        functools.partial(local, n_row, n_col, 5, 6, 4),
        mesh=mesh,
        in_specs=(both, both, P(), P("row", None, None), P("row")),
        out_specs=(both, P()),
        check_vma=False,
    )
```

```python
import functools

import jax
import jax.numpy as jnp
import ml_dtypes
import numpy as np
from jax import lax
from jax.experimental import pallas as pl
from jax.experimental.pallas import tpu as pltpu
from jax.sharding import PartitionSpec as P

SWEEPS = 12
ROUNDS = 2
TILE_R = 16
TILE_C = 128
screen_mu = 0.1
damping = 0.5


def spectral_tables(edge):
    k = np.arange(1, edge + 1)
    basis = np.sqrt(2.0 / (edge + 1)) * np.sin(np.pi * np.outer(k, k) / (edge + 1))
    line = 2.0 * np.cos(np.pi * k / (edge + 1))
    eig = (6.0 + screen_mu) - (line[:, None, None] + line[None, :, None] + line[None, None, :])
    c, h = 6.0 + screen_mu, 6.0
    g = c / h
    q = 1.0 / g
    u = np.zeros_like(eig)
    t = np.ones_like(eig)
    d = t / c
    for _ in range(SWEEPS):
        u = u + d
        t = t - eig * d
        q_new = 1.0 / (2.0 * g - q)
        d = q_new * q * d + (2.0 * q_new / h) * t
        q = q_new
    return basis, u.reshape(edge, edge * edge)


def two_parts(x):
    high = x.astype(ml_dtypes.bfloat16)
    return np.stack([high, (x - high.astype(np.float64)).astype(ml_dtypes.bfloat16)])


def split(x):
    high = x.astype(jnp.bfloat16)
    return high, (x - high.astype(jnp.float32)).astype(jnp.bfloat16)


def dot(a, b):
    return jnp.dot(a, b, preferred_element_type=jnp.float32)


def dot_split(a, b):
    (a_high, a_low), (b_high, b_low) = a, b
    return dot(a_high, b_high) + (dot(a_low, b_high) + dot(a_high, b_low))


def peers(n_col):
    side = int(round(n_col**0.5))
    steps = [(a, b) for a in range(side) for b in range(side) if a + b > 0]
    return side, sorted(steps, key=lambda p: -(min(p[0], side - p[0]) + min(p[1], side - p[1])))


def spread_kernel(
    n_row,
    n_col,
    S,
    tbl,
    orb_hbm,
    grad_hbm,
    kron_hbm,
    sx_hbm,
    poly_hbm,
    exb,
    energy_out,
    orb,
    grad,
    kron,
    sx,
    poly,
    box_stage,
    q_stage,
    slab0,
    q_slab,
    slab1,
    pack,
    pair_box,
    partner,
    density,
    term_stage,
    terms,
    wide,
    summed,
    final_stage,
    e_mine,
    e_group,
    e_sum,
    e_row,
    first_of,
    second_of,
    load_sem,
    send_sem,
    recv_sem,
):
    me = lax.axis_index("col")
    row = lax.axis_index("row")
    own, edge, plane = orb.shape
    norb = own * n_col
    slots = S * n_col
    halves = edge // TILE_R
    strips = plane // TILE_C

    loads = [
        pltpu.make_async_copy(a, b, load_sem.at[i])
        for i, (a, b) in enumerate(
            ((orb_hbm, orb), (grad_hbm, grad), (kron_hbm, kron), (sx_hbm, sx), (poly_hbm, poly))
        )
    ]
    for one in loads:
        one.start()

    barrier = pltpu.get_barrier_semaphore()

    def greet_col(d, _):
        pl.semaphore_signal(barrier, inc=1, device_id={"col": (me + d) % n_col}, device_id_type=pl.DeviceIdType.MESH)
        return 0

    def greet_row(d, _):
        pl.semaphore_signal(barrier, inc=1, device_id={"row": (row + d) % n_row}, device_id_type=pl.DeviceIdType.MESH)
        return 0

    lax.fori_loop(1, n_col, greet_col, 0)
    lax.fori_loop(1, n_row, greet_row, 0)

    count_at = n_col * 8
    offset_at = count_at + n_col

    def rank(r, firsts):
        def seek(p, state):
            start, found = state
            count = tbl[count_at + p]
            inside = (r >= start) & (r < start + count)
            return start + count, jnp.where(inside, p * 4 + r - start, found)

        total, found = lax.fori_loop(0, n_col, seek, (jnp.int32(0), jnp.int32(-1)))
        at = jnp.maximum(found, 0) * 2
        first = tbl[at]
        first_of[r] = first
        second_of[r] = tbl[at + 1]
        lane = lax.broadcasted_iota(jnp.int32, (norb, slots), 1)
        return jnp.where(lane == r, jnp.where(found >= 0, first, -1), firsts)

    firsts = lax.fori_loop(0, slots, rank, jnp.full((norb, slots), -1, jnp.int32))
    choose = (lax.broadcasted_iota(jnp.int32, (norb, slots), 0) == firsts).astype(jnp.float32).astype(jnp.bfloat16)

    def total_live(p, acc):
        return acc + tbl[count_at + p]

    live_total = lax.fori_loop(0, n_col, total_live, jnp.int32(0))

    def tile_of(s):
        return pl.ds(pl.multiple_of((s // strips) * TILE_R, TILE_R), TILE_R), pl.ds(
            pl.multiple_of((s % strips) * TILE_C, TILE_C), TILE_C
        )

    my_rows, my_cols = tile_of(me)

    def exchange(src_of, dst, which, before=None):
        side, steps = peers(n_col)
        for dy, dz in steps:
            to = ((me // side + dy) % side) * side + (me % side + dz) % side
            if before is not None:
                before(to)
            pltpu.make_async_remote_copy(
                src_ref=src_of(to),
                dst_ref=dst,
                send_sem=send_sem.at[which],
                recv_sem=recv_sem.at[which],
                device_id={"col": to},
                device_id_type=pl.DeviceIdType.MESH,
            ).start()
        if before is not None:
            before(me)
        pltpu.make_async_copy(src_of(me), dst, recv_sem.at[which]).start()

    def arrived(ref, which):
        pltpu.make_async_copy(ref, ref, recv_sem.at[which]).wait()

    def sent(ref, which):
        pltpu.make_async_copy(ref, ref, send_sem.at[which]).wait()

    loads[0].wait()
    box_stage[...] = orb[...].astype(jnp.bfloat16)
    pl.semaphore_wait(barrier, n_col - 1 + n_row - 1)

    def from_boxes(s):
        rows, cols = tile_of(s)
        return box_stage.at[:, rows, cols]

    def from_q(s):
        rows, cols = tile_of(s)
        return q_stage.at[:, rows, cols]

    mine4 = pl.ds(me * own, own)
    exchange(from_boxes, slab0.at[mine4], 0)
    loads[1].wait()
    q_stage[...] = orb[...] - damping * grad[...]
    exchange(from_q, q_slab.at[mine4], 1)
    for one in loads[2:]:
        one.wait()

    energies = []
    for r in range(ROUNDS):
        slab = (slab0, slab1)[r]
        if r == 0:
            arrived(slab0, 0)

        def fill(p):
            for k in range(S):
                pack[r, p * 2 * S + 2 * k] = slab[first_of[p * S + k]]
                pack[r, p * 2 * S + 2 * k + 1] = slab[second_of[p * S + k]]

        def from_pack(p):
            return pack.at[r, pl.ds(p * 2 * S, 2 * S)]

        exchange(from_pack, pair_box.at[r, :, my_rows, my_cols], 2 + 2 * r, fill)
        arrived(pair_box.at[r], 2 + 2 * r)

        lane = lax.broadcasted_iota(jnp.int32, (edge, plane), 1)
        line = lax.broadcasted_iota(jnp.int32, (edge, plane), 0)
        for k in range(S):
            a = offset_at + 3 * first_of[me * S + k]
            b = offset_at + 3 * second_of[me * S + k]
            dx = tbl[a] - tbl[b]
            dy = tbl[a + 1] - tbl[b + 1]
            dz = tbl[a + 2] - tbl[b + 2]
            t = dy * edge + dz
            moved = pair_box[r, 2 * k + 1].astype(jnp.float32)
            moved = pltpu.roll(moved, lax.rem(plane - t, jnp.int32(plane)), 1)
            moved = pltpu.roll(moved, lax.rem(edge - dx, jnp.int32(edge)), 0)
            at_x = line + dx
            at_y = lane // edge + dy
            at_z = lane % edge + dz
            inside = (
                (at_x >= 0) & (at_x < edge) & (at_y >= 0) & (at_y < edge) & (at_z >= 0) & (at_z < edge)
            )
            moved = jnp.where(inside, moved, 0.0)
            partner[pl.ds(k * edge, edge), :] = moved
            density[pl.ds(k * edge, edge), :] = pair_box[r, 2 * k].astype(jnp.float32) * moved

        yz = kron[0], kron[1]
        along_x = sx[0], sx[1]
        modes = dot_split(split(density[...]), yz)
        modes = dot_split(along_x, split(modes)).reshape(S, edge, plane) * poly[...][None]
        modes = dot_split(along_x, split(modes.reshape(S * edge, plane)))
        potential = dot_split(split(modes), yz)
        term_stage[r] = (potential * partner[...]).astype(jnp.bfloat16).reshape(S, edge, plane)
        cells = (density[...] * potential).reshape(S, edge, plane)
        energy = jnp.zeros((edge, plane), jnp.float32)
        for k in range(S):
            energy = energy + jnp.where(me * S + k < live_total, cells[k], 0.0)
        energies.append(energy)

        def from_terms(s):
            rows, cols = tile_of(s)
            return term_stage.at[r, :, rows, cols]

        exchange(from_terms, terms.at[r, pl.ds(me * S, S)], 3 + 2 * r)

        if r == ROUNDS - 1:
            for i, e in enumerate(energies):
                part = jnp.sum(e.reshape(edge // 8, 8, plane), axis=0)
                e_mine[i] = sum(part[:, c * TILE_C : (c + 1) * TILE_C] for c in range(strips))
            exchange(lambda s: e_mine, e_group.at[me], 7)

        arrived(terms.at[r], 3 + 2 * r)
        wide[...] = terms[r].astype(jnp.float32).reshape(slots * TILE_R, TILE_C)
        if r == 0:
            arrived(q_slab, 1)
        for j in range(TILE_R):
            part = wide[pl.ds(j, slots, stride=TILE_R), :].astype(jnp.bfloat16)
            out = dot(choose, part)
            if r == 0:
                summed[pl.ds(j, norb, stride=TILE_R), :] = out
            else:
                summed[pl.ds(j, norb, stride=TILE_R), :] += out
        if r == 0:
            total = summed[...].reshape(norb, TILE_R, TILE_C)
            slab1[...] = (q_slab[...] - damping * total).astype(jnp.bfloat16)
        else:
            final_stage[...] = summed[...].reshape(norb, TILE_R, TILE_C).astype(jnp.bfloat16)

    exchange(lambda s: final_stage.at[pl.ds(s * own, own)], exb.at[:, my_rows, my_cols], 6)

    arrived(e_group, 7)
    e_sum[...] = jnp.sum(e_group[...], axis=0)

    def go_row(d, _):
        pltpu.make_async_remote_copy(
            src_ref=e_sum,
            dst_ref=e_row.at[row],
            send_sem=send_sem.at[8],
            recv_sem=recv_sem.at[8],
            device_id={"row": (row + d) % n_row},
            device_id_type=pl.DeviceIdType.MESH,
        ).start()
        return 0

    lax.fori_loop(1, n_row, go_row, 0)
    pltpu.make_async_copy(e_sum, e_row.at[row], recv_sem.at[8]).start()
    arrived(e_row, 8)
    all_cells = edge * edge * edge * n_row * n_col
    for i in range(ROUNDS):
        energy_out[i] = jnp.sum(jnp.sum(e_row[:, i], axis=0)) / all_cells
    arrived(exb, 6)

    others = n_col - 1
    sent(slab0.at[pl.ds(0, others * own)], 0)
    sent(q_slab.at[pl.ds(0, others * own)], 1)
    for r in range(ROUNDS):
        sent(pack.at[r, pl.ds(0, others * 2 * S)], 2 + 2 * r)
        sent(terms.at[r, pl.ds(0, others * S)], 3 + 2 * r)
    sent(final_stage.at[pl.ds(0, others * own)], 6)
    sent(e_group.at[pl.ds(0, others)], 7)
    if n_row > 1:
        sent(e_row.at[pl.ds(0, n_row - 1)], 8)


def spread_pairs(n_row, n_col, S, orbitals, gradient, offsets, pairs, counts):
    own, edge, plane = orbitals.shape
    norb = own * n_col
    slots = S * n_col
    base = lax.axis_index("row") * norb
    table = jnp.concatenate(
        [
            (pairs - base).reshape(-1),
            counts,
            lax.dynamic_slice_in_dim(offsets, base, norb, 0).reshape(-1),
        ]
    )
    basis, poly = spectral_tables(edge)
    kron = two_parts(np.kron(basis, basis))
    sx = two_parts(np.kron(np.eye(S), basis))
    hbm = pl.BlockSpec(memory_space=pltpu.HBM)
    f32, bf16 = jnp.float32, jnp.bfloat16
    tiles = (norb, TILE_R, TILE_C)
    exchanged, energies = pl.pallas_call(
        functools.partial(spread_kernel, n_row, n_col, S),
        out_shape=(
            jax.ShapeDtypeStruct((own, edge, plane), bf16),
            jax.ShapeDtypeStruct((ROUNDS,), f32),
        ),
        in_specs=[pl.BlockSpec(memory_space=pltpu.SMEM)] + [hbm] * 5,
        out_specs=(pl.BlockSpec(memory_space=pltpu.VMEM), pl.BlockSpec(memory_space=pltpu.SMEM)),
        scratch_shapes=[
            pltpu.VMEM((own, edge, plane), f32),
            pltpu.VMEM((own, edge, plane), f32),
            pltpu.VMEM((2, plane, plane), bf16),
            pltpu.VMEM((2, S * edge, S * edge), bf16),
            pltpu.VMEM((edge, plane), f32),
            pltpu.VMEM((own, edge, plane), bf16),
            pltpu.VMEM((own, edge, plane), f32),
            pltpu.VMEM(tiles, bf16),
            pltpu.VMEM(tiles, f32),
            pltpu.VMEM(tiles, bf16),
            pltpu.VMEM((ROUNDS, slots * 2, TILE_R, TILE_C), bf16),
            pltpu.VMEM((ROUNDS, 2 * S, edge, plane), bf16),
            pltpu.VMEM((S * edge, plane), f32),
            pltpu.VMEM((S * edge, plane), f32),
            pltpu.VMEM((ROUNDS, S, edge, plane), bf16),
            pltpu.VMEM((ROUNDS, slots, TILE_R, TILE_C), bf16),
            pltpu.VMEM((slots * TILE_R, TILE_C), f32),
            pltpu.VMEM((norb * TILE_R, TILE_C), f32),
            pltpu.VMEM(tiles, bf16),
            pltpu.VMEM((ROUNDS, 8, TILE_C), f32),
            pltpu.VMEM((n_col, ROUNDS, 8, TILE_C), f32),
            pltpu.VMEM((ROUNDS, 8, TILE_C), f32),
            pltpu.VMEM((n_row, ROUNDS, 8, TILE_C), f32),
            pltpu.SMEM((slots,), jnp.int32),
            pltpu.SMEM((slots,), jnp.int32),
            pltpu.SemaphoreType.DMA((5,)),
            pltpu.SemaphoreType.DMA((9,)),
            pltpu.SemaphoreType.DMA((9,)),
        ],
        compiler_params=pltpu.CompilerParams(
            collective_id=S, has_side_effects=True, vmem_limit_bytes=60 * 1024 * 1024
        ),
    )(table, orbitals, gradient, jnp.asarray(kron), jnp.asarray(sx), jnp.asarray(poly.astype(np.float32)))
    updated = orbitals - gradient - damping * exchanged.astype(f32)
    return updated, energies


def flipped(x, edge):
    per_tile = TILE_C // edge
    tiles = x.shape[1] // TILE_C
    block = lax.broadcasted_iota(jnp.int32, (1, TILE_C), 1) // edge
    out = []
    for t in reversed(range(tiles)):
        tile = x[:, t * TILE_C : (t + 1) * TILE_C]
        step = per_tile // 2
        while step:
            back = pltpu.roll(tile, TILE_C - step * edge, 1)
            if 2 * step == per_tile:
                tile = back
            else:
                ahead = pltpu.roll(tile, step * edge, 1)
                tile = jnp.where(block // step % 2 == 0, back, ahead)
            step //= 2
        out.append(tile)
    return jnp.concatenate(out, 1)


def folded(basis, poly):
    edge = basis.shape[0]
    half = [np.kron(basis[i::2, : edge // 2].T, basis) for i in range(2)]
    kron = np.stack([two_parts(x) for x in half + [x.T for x in half]])
    poly = poly.reshape(edge, edge, edge)
    poly = np.concatenate([poly[:, 0::2], poly[:, 1::2]], 1)
    return kron, poly.reshape(edge, edge * edge)


def along_lanes(x, step):
    tiles = x.shape[1] // TILE_C
    left = step < 0
    turn = jnp.where(left, step + TILE_C, step)
    lane = lax.broadcasted_iota(jnp.int32, (1, TILE_C), 1)
    own = lane < TILE_C - turn
    back = lax.rem(TILE_C - turn, jnp.int32(TILE_C))
    turned = [pltpu.roll(x[:, t * TILE_C : (t + 1) * TILE_C], back, 1) for t in range(tiles)]
    before = own & left
    after = jnp.logical_not(own | left)
    out = []
    for t in range(tiles):
        tile = turned[t]
        tile = jnp.where(before, turned[t - 1], tile) if t > 0 else tile
        out.append(jnp.where(after, turned[t + 1], tile) if t < tiles - 1 else tile)
    return jnp.concatenate(out, 1)


def direct_kernel(
    n_row,
    n_col,
    REMOTE,
    LOCAL,
    pairs_hbm,
    counts_hbm,
    offsets_hbm,
    orb_hbm,
    grad_hbm,
    kron_hbm,
    sx_hbm,
    poly_hbm,
    updated_hbm,
    energy_out,
    over_out,
    exchanged,
    pairs,
    counts,
    offsets,
    orb,
    grad,
    kron,
    sx,
    poly,
    stage0,
    stage1,
    slab0,
    slab1,
    pack,
    pair_box,
    partner,
    density,
    e_mine,
    e_group,
    e_sum,
    e_row,
    slot_rows,
    slot_of,
    load_sem,
    slot_sem,
    send_sem,
    recv_sem,
):
    me = lax.axis_index("col")
    row = lax.axis_index("row")
    own, edge, plane = orb.shape
    norb = own * n_col
    base = row * norb
    strips = plane // TILE_C
    per_owner = pairs.shape[0]
    mesh_id = pl.DeviceIdType.MESH
    box_stage, slab = (stage0, stage1), (slab0, slab1)

    barrier = pltpu.get_barrier_semaphore()
    side, steps = peers(n_col)

    def peer(step):
        return ((me // side + step[0]) % side) * side + (me % side + step[1]) % side

    for step in steps:
        pl.semaphore_signal(barrier, inc=1, device_id={"col": peer(step)}, device_id_type=mesh_id)

    def greet_row(d, _):
        pl.semaphore_signal(barrier, inc=1, device_id={"row": (row + d) % n_row}, device_id_type=mesh_id)
        return 0

    lax.fori_loop(1, n_row, greet_row, 0)

    sources = (pairs_hbm, counts_hbm, offsets_hbm, orb_hbm, grad_hbm, kron_hbm, sx_hbm, poly_hbm)
    loads = [
        pltpu.make_async_copy(a, b, load_sem.at[i])
        for i, (a, b) in enumerate(zip(sources, (pairs, counts, offsets, orb, grad, kron, sx, poly)))
    ]
    for one in loads[:4]:
        one.start()
    for one in loads[:3]:
        one.wait()

    lane = lax.broadcasted_iota(jnp.int32, (8, TILE_C), 1)

    def place(index, state):
        p, k = index // per_owner, index % per_owner
        at_first = lax.div(pairs[k, 0, p] - base, jnp.int32(own))
        at_second = lax.div(pairs[k, 1, p] - base, jnp.int32(own))
        here = jnp.where(k < counts[p], at_first, -1)
        far = jnp.where(at_first == at_second, -1, here)
        near = jnp.where(at_first == at_second, here, -1)
        out = []
        for device, (count, slots) in zip((far, near), state):
            hit = lane == device
            slots = tuple(jnp.where(hit & (count == s), index, held) for s, held in enumerate(slots))
            out.append((count + hit.astype(jnp.int32), slots))
        return tuple(out)

    none = jnp.full((8, TILE_C), -1, jnp.int32)
    zero = jnp.zeros((8, TILE_C), jnp.int32)
    (far_count, far_slots), (near_count, near_slots) = lax.fori_loop(
        0, n_col * per_owner, place, ((zero, (none,) * REMOTE), (zero, (none,) * LOCAL))
    )
    for s, held in enumerate(far_slots + near_slots):
        slot_rows[pl.ds(s, 1), :] = held[0:1, :]
    over = ((far_count > REMOTE) | (near_count > LOCAL)).astype(jnp.float32)
    overflow = jnp.sum(over[0:1, :], axis=1, keepdims=True)
    to_scalars = pltpu.make_async_copy(slot_rows, slot_of, slot_sem.at[0])
    to_scalars.start()

    def tile_of(s):
        return pl.ds(pl.multiple_of((s // strips) * TILE_R, TILE_R), TILE_R), pl.ds(
            pl.multiple_of((s % strips) * TILE_C, TILE_C), TILE_C
        )

    my_rows, my_cols = tile_of(me)

    def send(src, dst, which, to):
        pltpu.make_async_remote_copy(
            src_ref=src,
            dst_ref=dst,
            send_sem=send_sem.at[which],
            recv_sem=recv_sem.at[which],
            device_id={"col": to},
            device_id_type=mesh_id,
        ).start()

    def arrived(ref, which):
        pltpu.make_async_copy(ref, ref, recv_sem.at[which]).wait()

    def sent(ref, which):
        pltpu.make_async_copy(ref, ref, send_sem.at[which]).wait()

    def send_boxes(r):
        def part(s):
            rows, cols = tile_of(s)
            return box_stage[r].at[:, rows, cols]

        dst = slab[r].at[pl.ds(me * own, own)]
        for step in steps:
            send(part(peer(step)), dst, 2 * r, peer(step))
        pltpu.make_async_copy(part(me), dst, recv_sem.at[2 * r]).start()

    def send_pairs(r):
        dst = pair_box.at[r, :, my_rows, my_cols]

        def fill(to):
            for s in range(REMOTE):
                index = jnp.maximum(slot_of[s, to], 0)
                second = pairs[lax.rem(index, jnp.int32(per_owner)), 1, lax.div(index, jnp.int32(per_owner))]
                pack[r, to, s] = slab[r][jnp.clip(second - base, 0, norb - 1)]

        for step in steps:
            fill(peer(step))
            send(pack.at[r, peer(step)], dst, 2 * r + 1, peer(step))
        fill(me)
        pltpu.make_async_copy(pack.at[r, me], dst, recv_sem.at[2 * r + 1]).start()

    line = lax.broadcasted_iota(jnp.int32, (edge, 1), 0)
    cell = lax.broadcasted_iota(jnp.int32, (1, plane), 1)

    def work(r, start, number, between=None):
        firsts = []
        for n in range(number):
            code = slot_of[start + n, me]
            index = jnp.maximum(code, 0)
            p = lax.div(index, jnp.int32(per_owner))
            k = lax.rem(index, jnp.int32(per_owner))
            first, second = pairs[k, 0, p], pairs[k, 1, p]
            mine = jnp.clip(first - base - me * own, 0, own - 1)
            firsts.append(jnp.where(code >= 0, mine, -1))
            dx = offsets[0, first] - offsets[0, second]
            dy = offsets[1, first] - offsets[1, second]
            dz = offsets[2, first] - offsets[2, second]
            t = dy * edge + dz
            if start < REMOTE:
                moved = pair_box[r, start + n]
            else:
                moved = box_stage[r][jnp.clip(second - base - me * own, 0, own - 1)]
            moved = moved.astype(jnp.float32)
            moved = along_lanes(moved, t)
            moved = pltpu.roll(moved, lax.rem(edge - dx, jnp.int32(edge)), 0)
            at_x = line + dx
            at_y = cell // edge + dy
            at_z = cell % edge + dz
            inside_x = ((at_x >= 0) & (at_x < edge)).astype(jnp.float32)
            inside_yz = ((at_y >= 0) & (at_y < edge) & (at_z >= 0) & (at_z < edge)).astype(jnp.float32)
            moved = moved * inside_yz * inside_x
            partner[pl.ds(n * edge, edge), :] = moved
            density[pl.ds(n * edge, edge), :] = box_stage[r][mine].astype(jnp.float32) * moved
        rows = number * edge

        def halves(x, which):
            high, low = split(x)
            both = dot(jnp.concatenate([high, low], 0), kron[which, 0])
            return both[:rows] + (both[rows:] + dot(high, kron[which, 1]))

        def to_modes(x):
            near, far = x[:, : plane // 2], flipped(x[:, plane // 2 :], edge)
            return jnp.concatenate([halves(near + far, 0), halves(near - far, 1)], 1)

        def to_cells(x):
            even, odd = halves(x[:, : plane // 2], 2), halves(x[:, plane // 2 :], 3)
            return jnp.concatenate([even + odd, flipped(even - odd, edge)], 1)

        def along_x(x):
            high, low = split(x)
            part = sx[0, pl.ds(0, rows), pl.ds(0, rows)]
            both = dot(jnp.concatenate([part, sx[1, pl.ds(0, rows), pl.ds(0, rows)]], 0), high)
            return both[:rows] + (both[rows:] + dot(part, low))

        def energy_of(modes, scaled):
            energy = jnp.zeros((8, TILE_C), jnp.float32)
            for n in range(number):
                part = jnp.sum((modes[n] * scaled[n]).reshape(edge // 8, 8, plane), axis=0)
                part = sum(part[:, c * TILE_C : (c + 1) * TILE_C] for c in range(strips))
                energy = energy + jnp.where(firsts[n] >= 0, part, 0.0)
            return energy

        if between is not None:
            x = density[pl.ds(0, rows), :]
            near, far = x[:, : plane // 2], flipped(x[:, plane // 2 :], edge)
            modes = jnp.concatenate(
                [dot(y.astype(jnp.bfloat16), kron[i, 0]).astype(jnp.bfloat16) for i, y in enumerate((near + far, near - far))], 1
            )
            modes = dot(sx[0, pl.ds(0, rows), pl.ds(0, rows)], modes).reshape(number, edge, plane)
            between(energy_of(modes, modes * poly[...][None]))
        modes = along_x(to_modes(density[pl.ds(0, rows), :])).reshape(number, edge, plane)
        scaled = modes * poly[...][None]
        energy = energy_of(modes, scaled) if between is None else None
        potential = to_cells(along_x(scaled.reshape(rows, plane)))
        terms = (potential * partner[pl.ds(0, rows), :]).astype(jnp.bfloat16).astype(jnp.float32)
        for o in range(own):
            total = exchanged[o]
            for n in range(number):
                total = total + jnp.where(firsts[n] == o, terms[n * edge : (n + 1) * edge], 0.0)
            exchanged[o] = total
        return energy

    exchanged[...] = jnp.zeros_like(exchanged)
    loads[3].wait()
    for one in loads[4:]:
        one.start()
    box_stage[0][...] = orb[...].astype(jnp.bfloat16)
    pl.semaphore_wait(barrier, n_col - 1 + n_row - 1)
    send_boxes(0)
    to_scalars.wait()
    for one in loads[4:]:
        one.wait()

    def total_of(energy):
        return jnp.sum(jnp.sum(energy, axis=0, keepdims=True), axis=1, keepdims=True)

    half = LOCAL // 2
    kept = []
    for r in range(ROUNDS):
        energy = work(r, REMOTE, half)
        arrived(slab[r], 2 * r)
        send_pairs(r)
        energy = energy + work(r, REMOTE + half, LOCAL - half)
        arrived(pair_box.at[r], 2 * r + 1)
        if r < ROUNDS - 1:
            kept.append(total_of(energy + work(r, 0, REMOTE)))
            box_stage[r + 1][...] = (orb[...] - damping * ((r + 1.0) * grad[...] + exchanged[...])).astype(jnp.bfloat16)
            send_boxes(r + 1)
        else:

            def send_energy(last):
                values = kept + [total_of(energy + last), overflow]
                at = lax.broadcasted_iota(jnp.int32, (1, TILE_C), 1)
                out = jnp.zeros((1, TILE_C), jnp.float32)
                for i, value in enumerate(values):
                    out = jnp.where(at == i, value, out)
                e_mine[...] = out
                for step in steps:
                    send(e_mine, e_group.at[me], 2 * ROUNDS, peer(step))
                pltpu.make_async_copy(e_mine, e_group.at[me], recv_sem.at[2 * ROUNDS]).start()

            work(r, 0, REMOTE, send_energy)

    orb[...] = orb[...] - damping * (ROUNDS * grad[...] + exchanged[...])
    store = pltpu.make_async_copy(orb, updated_hbm, slot_sem.at[0])
    store.start()

    arrived(e_group, 2 * ROUNDS)
    e_sum[...] = jnp.sum(e_group[...], axis=0)
    last = 2 * ROUNDS + 1

    def go_row(d, _):
        pltpu.make_async_remote_copy(
            src_ref=e_sum,
            dst_ref=e_row.at[row],
            send_sem=send_sem.at[last],
            recv_sem=recv_sem.at[last],
            device_id={"row": (row + d) % n_row},
            device_id_type=mesh_id,
        ).start()
        return 0

    lax.fori_loop(1, n_row, go_row, 0)
    pltpu.make_async_copy(e_sum, e_row.at[row], recv_sem.at[last]).start()
    others = n_col - 1
    for r in range(ROUNDS):
        sent(slab[r].at[pl.ds(0, others * own)], 2 * r)
        sent(pack.at[r, pl.ds(0, others)], 2 * r + 1)
    sent(e_group.at[pl.ds(0, others)], 2 * ROUNDS)
    store.wait()
    arrived(e_row, last)
    values = jnp.sum(e_row[...], axis=0)
    at = lax.broadcasted_iota(jnp.int32, (1, TILE_C), 1)
    for i in range(ROUNDS):
        energy_out[i] = jnp.sum(jnp.where(at == i, values, 0.0)) / (edge * edge * edge * n_row * n_col)
    over_out[0] = jnp.sum(jnp.where(at == ROUNDS, values, 0.0))
    if n_row > 1:
        sent(e_row.at[pl.ds(0, n_row - 1)], last)


def direct_pairs(n_row, n_col, REMOTE, LOCAL, orbitals, gradient, offsets, pairs, counts):
    own, edge, plane = orbitals.shape
    norb = own * n_col
    basis, poly = spectral_tables(edge)
    kron, poly = folded(basis, poly)
    most = max(REMOTE, LOCAL - LOCAL // 2)
    sx = two_parts(np.kron(np.eye(most), basis))
    smem = pl.BlockSpec(memory_space=pltpu.SMEM)
    f32, bf16 = jnp.float32, jnp.bfloat16
    return pl.pallas_call(
        functools.partial(direct_kernel, n_row, n_col, REMOTE, LOCAL),
        out_shape=(
            jax.ShapeDtypeStruct((own, edge, plane), f32),
            jax.ShapeDtypeStruct((ROUNDS,), f32),
            jax.ShapeDtypeStruct((1,), f32),
        ),
        in_specs=[pl.BlockSpec(memory_space=pl.ANY)] * 8,
        out_specs=(pl.BlockSpec(memory_space=pl.ANY), smem, smem),
        scratch_shapes=[
            pltpu.VMEM((own, edge, plane), f32),
            pltpu.SMEM((pairs.shape[1], 2, n_col), jnp.int32),
            pltpu.SMEM((n_col,), jnp.int32),
            pltpu.SMEM((3, offsets.shape[0]), jnp.int32),
            pltpu.VMEM((own, edge, plane), f32),
            pltpu.VMEM((own, edge, plane), f32),
            pltpu.VMEM((4, 2, plane // 2, plane // 2), bf16),
            pltpu.VMEM((2, most * edge, most * edge), bf16),
            pltpu.VMEM((edge, plane), f32),
            pltpu.VMEM((own, edge, plane), bf16),
            pltpu.VMEM((own, edge, plane), bf16),
            pltpu.VMEM((norb, TILE_R, TILE_C), bf16),
            pltpu.VMEM((norb, TILE_R, TILE_C), bf16),
            pltpu.VMEM((ROUNDS, n_col, REMOTE, TILE_R, TILE_C), bf16),
            pltpu.VMEM((ROUNDS, REMOTE, edge, plane), bf16),
            pltpu.VMEM((most * edge, plane), f32),
            pltpu.VMEM((most * edge, plane), f32),
            pltpu.VMEM((1, TILE_C), f32),
            pltpu.VMEM((n_col, 1, TILE_C), f32),
            pltpu.VMEM((1, TILE_C), f32),
            pltpu.VMEM((n_row, 1, TILE_C), f32),
            pltpu.VMEM((16, TILE_C), jnp.int32),
            pltpu.SMEM((16, TILE_C), jnp.int32),
            pltpu.SemaphoreType.DMA((8,)),
            pltpu.SemaphoreType.DMA((1,)),
            pltpu.SemaphoreType.DMA((2 * ROUNDS + 2,)),
            pltpu.SemaphoreType.DMA((2 * ROUNDS + 2,)),
        ],
        compiler_params=pltpu.CompilerParams(
            collective_id=1, has_side_effects=True, vmem_limit_bytes=60 * 1024 * 1024
        ),
    )(
        pairs.transpose(1, 2, 0),
        counts,
        offsets.T,
        orbitals,
        gradient,
        jnp.asarray(kron),
        jnp.asarray(sx),
        jnp.asarray(poly.astype(np.float32)),
    )


def local(n_row, n_col, REMOTE, LOCAL, S, orbitals, gradient, offsets, pairs, counts):
    updated, energies, over = direct_pairs(n_row, n_col, REMOTE, LOCAL, orbitals, gradient, offsets, pairs, counts)

    def enough():
        return updated, energies

    def general():
        return spread_pairs(n_row, n_col, S, orbitals, gradient, offsets, pairs, counts)

    return lax.cond(over[0] > 0, general, enough)


def solution(mesh):
    n_row, n_col = mesh.shape["row"], mesh.shape["col"]
    both = P(("row", "col"), None, None)
    return jax.shard_map(
        functools.partial(local, n_row, n_col, 5, 6, 4),
        mesh=mesh,
        in_specs=(both, both, P(), P("row", None, None), P("row")),
        out_specs=(both, P()),
        check_vma=False,
    )
```

```python
import functools

import jax
import jax.numpy as jnp
import ml_dtypes
import numpy as np
from jax import lax
from jax.experimental import pallas as pl
from jax.experimental.pallas import tpu as pltpu
from jax.sharding import PartitionSpec as P

SWEEPS = 12
ROUNDS = 2
TILE_R = 16
TILE_C = 128
screen_mu = 0.1
damping = 0.5


def spectral_tables(edge):
    k = np.arange(1, edge + 1)
    basis = np.sqrt(2.0 / (edge + 1)) * np.sin(np.pi * np.outer(k, k) / (edge + 1))
    line = 2.0 * np.cos(np.pi * k / (edge + 1))
    eig = (6.0 + screen_mu) - (line[:, None, None] + line[None, :, None] + line[None, None, :])
    c, h = 6.0 + screen_mu, 6.0
    g = c / h
    q = 1.0 / g
    u = np.zeros_like(eig)
    t = np.ones_like(eig)
    d = t / c
    for _ in range(SWEEPS):
        u = u + d
        t = t - eig * d
        q_new = 1.0 / (2.0 * g - q)
        d = q_new * q * d + (2.0 * q_new / h) * t
        q = q_new
    return basis, u.reshape(edge, edge * edge)


def two_parts(x):
    high = x.astype(ml_dtypes.bfloat16)
    return np.stack([high, (x - high.astype(np.float64)).astype(ml_dtypes.bfloat16)])


def split(x):
    high = x.astype(jnp.bfloat16)
    return high, (x - high.astype(jnp.float32)).astype(jnp.bfloat16)


def dot(a, b):
    return jnp.dot(a, b, preferred_element_type=jnp.float32)


def dot_split(a, b):
    (a_high, a_low), (b_high, b_low) = a, b
    return dot(a_high, b_high) + (dot(a_low, b_high) + dot(a_high, b_low))


def peers(n_col):
    side = int(round(n_col**0.5))
    steps = [(a, b) for a in range(side) for b in range(side) if a + b > 0]
    return side, sorted(steps, key=lambda p: -(min(p[0], side - p[0]) + min(p[1], side - p[1])))


def spread_kernel(
    n_row,
    n_col,
    S,
    tbl,
    orb_hbm,
    grad_hbm,
    kron_hbm,
    sx_hbm,
    poly_hbm,
    exb,
    energy_out,
    orb,
    grad,
    kron,
    sx,
    poly,
    box_stage,
    q_stage,
    slab0,
    q_slab,
    slab1,
    pack,
    pair_box,
    partner,
    density,
    term_stage,
    terms,
    wide,
    summed,
    final_stage,
    e_mine,
    e_group,
    e_sum,
    e_row,
    first_of,
    second_of,
    load_sem,
    send_sem,
    recv_sem,
):
    me = lax.axis_index("col")
    row = lax.axis_index("row")
    own, edge, plane = orb.shape
    norb = own * n_col
    slots = S * n_col
    halves = edge // TILE_R
    strips = plane // TILE_C

    loads = [
        pltpu.make_async_copy(a, b, load_sem.at[i])
        for i, (a, b) in enumerate(
            ((orb_hbm, orb), (grad_hbm, grad), (kron_hbm, kron), (sx_hbm, sx), (poly_hbm, poly))
        )
    ]
    for one in loads:
        one.start()

    barrier = pltpu.get_barrier_semaphore()

    def greet_col(d, _):
        pl.semaphore_signal(barrier, inc=1, device_id={"col": (me + d) % n_col}, device_id_type=pl.DeviceIdType.MESH)
        return 0

    def greet_row(d, _):
        pl.semaphore_signal(barrier, inc=1, device_id={"row": (row + d) % n_row}, device_id_type=pl.DeviceIdType.MESH)
        return 0

    lax.fori_loop(1, n_col, greet_col, 0)
    lax.fori_loop(1, n_row, greet_row, 0)

    count_at = n_col * 8
    offset_at = count_at + n_col

    def rank(r, firsts):
        def seek(p, state):
            start, found = state
            count = tbl[count_at + p]
            inside = (r >= start) & (r < start + count)
            return start + count, jnp.where(inside, p * 4 + r - start, found)

        total, found = lax.fori_loop(0, n_col, seek, (jnp.int32(0), jnp.int32(-1)))
        at = jnp.maximum(found, 0) * 2
        first = tbl[at]
        first_of[r] = first
        second_of[r] = tbl[at + 1]
        lane = lax.broadcasted_iota(jnp.int32, (norb, slots), 1)
        return jnp.where(lane == r, jnp.where(found >= 0, first, -1), firsts)

    firsts = lax.fori_loop(0, slots, rank, jnp.full((norb, slots), -1, jnp.int32))
    choose = (lax.broadcasted_iota(jnp.int32, (norb, slots), 0) == firsts).astype(jnp.float32).astype(jnp.bfloat16)

    def total_live(p, acc):
        return acc + tbl[count_at + p]

    live_total = lax.fori_loop(0, n_col, total_live, jnp.int32(0))

    def tile_of(s):
        return pl.ds(pl.multiple_of((s // strips) * TILE_R, TILE_R), TILE_R), pl.ds(
            pl.multiple_of((s % strips) * TILE_C, TILE_C), TILE_C
        )

    my_rows, my_cols = tile_of(me)

    def exchange(src_of, dst, which, before=None):
        side, steps = peers(n_col)
        for dy, dz in steps:
            to = ((me // side + dy) % side) * side + (me % side + dz) % side
            if before is not None:
                before(to)
            pltpu.make_async_remote_copy(
                src_ref=src_of(to),
                dst_ref=dst,
                send_sem=send_sem.at[which],
                recv_sem=recv_sem.at[which],
                device_id={"col": to},
                device_id_type=pl.DeviceIdType.MESH,
            ).start()
        if before is not None:
            before(me)
        pltpu.make_async_copy(src_of(me), dst, recv_sem.at[which]).start()

    def arrived(ref, which):
        pltpu.make_async_copy(ref, ref, recv_sem.at[which]).wait()

    def sent(ref, which):
        pltpu.make_async_copy(ref, ref, send_sem.at[which]).wait()

    loads[0].wait()
    box_stage[...] = orb[...].astype(jnp.bfloat16)
    pl.semaphore_wait(barrier, n_col - 1 + n_row - 1)

    def from_boxes(s):
        rows, cols = tile_of(s)
        return box_stage.at[:, rows, cols]

    def from_q(s):
        rows, cols = tile_of(s)
        return q_stage.at[:, rows, cols]

    mine4 = pl.ds(me * own, own)
    exchange(from_boxes, slab0.at[mine4], 0)
    loads[1].wait()
    q_stage[...] = orb[...] - damping * grad[...]
    exchange(from_q, q_slab.at[mine4], 1)
    for one in loads[2:]:
        one.wait()

    energies = []
    for r in range(ROUNDS):
        slab = (slab0, slab1)[r]
        if r == 0:
            arrived(slab0, 0)

        def fill(p):
            for k in range(S):
                pack[r, p * 2 * S + 2 * k] = slab[first_of[p * S + k]]
                pack[r, p * 2 * S + 2 * k + 1] = slab[second_of[p * S + k]]

        def from_pack(p):
            return pack.at[r, pl.ds(p * 2 * S, 2 * S)]

        exchange(from_pack, pair_box.at[r, :, my_rows, my_cols], 2 + 2 * r, fill)
        arrived(pair_box.at[r], 2 + 2 * r)

        lane = lax.broadcasted_iota(jnp.int32, (edge, plane), 1)
        line = lax.broadcasted_iota(jnp.int32, (edge, plane), 0)
        for k in range(S):
            a = offset_at + 3 * first_of[me * S + k]
            b = offset_at + 3 * second_of[me * S + k]
            dx = tbl[a] - tbl[b]
            dy = tbl[a + 1] - tbl[b + 1]
            dz = tbl[a + 2] - tbl[b + 2]
            t = dy * edge + dz
            moved = pair_box[r, 2 * k + 1].astype(jnp.float32)
            moved = pltpu.roll(moved, lax.rem(plane - t, jnp.int32(plane)), 1)
            moved = pltpu.roll(moved, lax.rem(edge - dx, jnp.int32(edge)), 0)
            at_x = line + dx
            at_y = lane // edge + dy
            at_z = lane % edge + dz
            inside = (
                (at_x >= 0) & (at_x < edge) & (at_y >= 0) & (at_y < edge) & (at_z >= 0) & (at_z < edge)
            )
            moved = jnp.where(inside, moved, 0.0)
            partner[pl.ds(k * edge, edge), :] = moved
            density[pl.ds(k * edge, edge), :] = pair_box[r, 2 * k].astype(jnp.float32) * moved

        yz = kron[0], kron[1]
        along_x = sx[0], sx[1]
        modes = dot_split(split(density[...]), yz)
        modes = dot_split(along_x, split(modes)).reshape(S, edge, plane) * poly[...][None]
        modes = dot_split(along_x, split(modes.reshape(S * edge, plane)))
        potential = dot_split(split(modes), yz)
        term_stage[r] = (potential * partner[...]).astype(jnp.bfloat16).reshape(S, edge, plane)
        cells = (density[...] * potential).reshape(S, edge, plane)
        energy = jnp.zeros((edge, plane), jnp.float32)
        for k in range(S):
            energy = energy + jnp.where(me * S + k < live_total, cells[k], 0.0)
        energies.append(energy)

        def from_terms(s):
            rows, cols = tile_of(s)
            return term_stage.at[r, :, rows, cols]

        exchange(from_terms, terms.at[r, pl.ds(me * S, S)], 3 + 2 * r)

        if r == ROUNDS - 1:
            for i, e in enumerate(energies):
                part = jnp.sum(e.reshape(edge // 8, 8, plane), axis=0)
                e_mine[i] = sum(part[:, c * TILE_C : (c + 1) * TILE_C] for c in range(strips))
            exchange(lambda s: e_mine, e_group.at[me], 7)

        arrived(terms.at[r], 3 + 2 * r)
        wide[...] = terms[r].astype(jnp.float32).reshape(slots * TILE_R, TILE_C)
        if r == 0:
            arrived(q_slab, 1)
        for j in range(TILE_R):
            part = wide[pl.ds(j, slots, stride=TILE_R), :].astype(jnp.bfloat16)
            out = dot(choose, part)
            if r == 0:
                summed[pl.ds(j, norb, stride=TILE_R), :] = out
            else:
                summed[pl.ds(j, norb, stride=TILE_R), :] += out
        if r == 0:
            total = summed[...].reshape(norb, TILE_R, TILE_C)
            slab1[...] = (q_slab[...] - damping * total).astype(jnp.bfloat16)
        else:
            final_stage[...] = summed[...].reshape(norb, TILE_R, TILE_C).astype(jnp.bfloat16)

    exchange(lambda s: final_stage.at[pl.ds(s * own, own)], exb.at[:, my_rows, my_cols], 6)

    arrived(e_group, 7)
    e_sum[...] = jnp.sum(e_group[...], axis=0)

    def go_row(d, _):
        pltpu.make_async_remote_copy(
            src_ref=e_sum,
            dst_ref=e_row.at[row],
            send_sem=send_sem.at[8],
            recv_sem=recv_sem.at[8],
            device_id={"row": (row + d) % n_row},
            device_id_type=pl.DeviceIdType.MESH,
        ).start()
        return 0

    lax.fori_loop(1, n_row, go_row, 0)
    pltpu.make_async_copy(e_sum, e_row.at[row], recv_sem.at[8]).start()
    arrived(e_row, 8)
    all_cells = edge * edge * edge * n_row * n_col
    for i in range(ROUNDS):
        energy_out[i] = jnp.sum(jnp.sum(e_row[:, i], axis=0)) / all_cells
    arrived(exb, 6)

    others = n_col - 1
    sent(slab0.at[pl.ds(0, others * own)], 0)
    sent(q_slab.at[pl.ds(0, others * own)], 1)
    for r in range(ROUNDS):
        sent(pack.at[r, pl.ds(0, others * 2 * S)], 2 + 2 * r)
        sent(terms.at[r, pl.ds(0, others * S)], 3 + 2 * r)
    sent(final_stage.at[pl.ds(0, others * own)], 6)
    sent(e_group.at[pl.ds(0, others)], 7)
    if n_row > 1:
        sent(e_row.at[pl.ds(0, n_row - 1)], 8)


def spread_pairs(n_row, n_col, S, orbitals, gradient, offsets, pairs, counts):
    own, edge, plane = orbitals.shape
    norb = own * n_col
    slots = S * n_col
    base = lax.axis_index("row") * norb
    table = jnp.concatenate(
        [
            (pairs - base).reshape(-1),
            counts,
            lax.dynamic_slice_in_dim(offsets, base, norb, 0).reshape(-1),
        ]
    )
    basis, poly = spectral_tables(edge)
    kron = two_parts(np.kron(basis, basis))
    sx = two_parts(np.kron(np.eye(S), basis))
    hbm = pl.BlockSpec(memory_space=pltpu.HBM)
    f32, bf16 = jnp.float32, jnp.bfloat16
    tiles = (norb, TILE_R, TILE_C)
    exchanged, energies = pl.pallas_call(
        functools.partial(spread_kernel, n_row, n_col, S),
        out_shape=(
            jax.ShapeDtypeStruct((own, edge, plane), bf16),
            jax.ShapeDtypeStruct((ROUNDS,), f32),
        ),
        in_specs=[pl.BlockSpec(memory_space=pltpu.SMEM)] + [hbm] * 5,
        out_specs=(pl.BlockSpec(memory_space=pltpu.VMEM), pl.BlockSpec(memory_space=pltpu.SMEM)),
        scratch_shapes=[
            pltpu.VMEM((own, edge, plane), f32),
            pltpu.VMEM((own, edge, plane), f32),
            pltpu.VMEM((2, plane, plane), bf16),
            pltpu.VMEM((2, S * edge, S * edge), bf16),
            pltpu.VMEM((edge, plane), f32),
            pltpu.VMEM((own, edge, plane), bf16),
            pltpu.VMEM((own, edge, plane), f32),
            pltpu.VMEM(tiles, bf16),
            pltpu.VMEM(tiles, f32),
            pltpu.VMEM(tiles, bf16),
            pltpu.VMEM((ROUNDS, slots * 2, TILE_R, TILE_C), bf16),
            pltpu.VMEM((ROUNDS, 2 * S, edge, plane), bf16),
            pltpu.VMEM((S * edge, plane), f32),
            pltpu.VMEM((S * edge, plane), f32),
            pltpu.VMEM((ROUNDS, S, edge, plane), bf16),
            pltpu.VMEM((ROUNDS, slots, TILE_R, TILE_C), bf16),
            pltpu.VMEM((slots * TILE_R, TILE_C), f32),
            pltpu.VMEM((norb * TILE_R, TILE_C), f32),
            pltpu.VMEM(tiles, bf16),
            pltpu.VMEM((ROUNDS, 8, TILE_C), f32),
            pltpu.VMEM((n_col, ROUNDS, 8, TILE_C), f32),
            pltpu.VMEM((ROUNDS, 8, TILE_C), f32),
            pltpu.VMEM((n_row, ROUNDS, 8, TILE_C), f32),
            pltpu.SMEM((slots,), jnp.int32),
            pltpu.SMEM((slots,), jnp.int32),
            pltpu.SemaphoreType.DMA((5,)),
            pltpu.SemaphoreType.DMA((9,)),
            pltpu.SemaphoreType.DMA((9,)),
        ],
        compiler_params=pltpu.CompilerParams(
            collective_id=S, has_side_effects=True, vmem_limit_bytes=60 * 1024 * 1024
        ),
    )(table, orbitals, gradient, jnp.asarray(kron), jnp.asarray(sx), jnp.asarray(poly.astype(np.float32)))
    updated = orbitals - gradient - damping * exchanged.astype(f32)
    return updated, energies


def flipped(x, edge):
    per_tile = TILE_C // edge
    tiles = x.shape[1] // TILE_C
    block = lax.broadcasted_iota(jnp.int32, (1, TILE_C), 1) // edge
    out = []
    for t in reversed(range(tiles)):
        tile = x[:, t * TILE_C : (t + 1) * TILE_C]
        step = per_tile // 2
        while step:
            back = pltpu.roll(tile, TILE_C - step * edge, 1)
            if 2 * step == per_tile:
                tile = back
            else:
                ahead = pltpu.roll(tile, step * edge, 1)
                tile = jnp.where(block // step % 2 == 0, back, ahead)
            step //= 2
        out.append(tile)
    return jnp.concatenate(out, 1)


def folded(basis, poly):
    edge = basis.shape[0]
    half = [np.kron(basis[i::2, : edge // 2].T, basis) for i in range(2)]
    kron = np.stack([two_parts(x) for x in half + [x.T for x in half]])
    poly = poly.reshape(edge, edge, edge)
    poly = np.concatenate([poly[:, 0::2], poly[:, 1::2]], 1)
    return kron, poly.reshape(edge, edge * edge)


def along_lanes(x, step):
    tiles = x.shape[1] // TILE_C
    left = step < 0
    turn = jnp.where(left, step + TILE_C, step)
    lane = lax.broadcasted_iota(jnp.int32, (1, TILE_C), 1)
    own = lane < TILE_C - turn
    back = lax.rem(TILE_C - turn, jnp.int32(TILE_C))
    turned = [pltpu.roll(x[:, t * TILE_C : (t + 1) * TILE_C], back, 1) for t in range(tiles)]
    before = own & left
    after = jnp.logical_not(own | left)
    out = []
    for t in range(tiles):
        tile = turned[t]
        tile = jnp.where(before, turned[t - 1], tile) if t > 0 else tile
        out.append(jnp.where(after, turned[t + 1], tile) if t < tiles - 1 else tile)
    return jnp.concatenate(out, 1)


def direct_kernel(
    n_row,
    n_col,
    REMOTE,
    LOCAL,
    pairs_hbm,
    counts_hbm,
    offsets_hbm,
    orb_hbm,
    grad_hbm,
    kron_hbm,
    sx_hbm,
    poly_hbm,
    updated_hbm,
    energy_out,
    over_out,
    exchanged,
    pairs,
    counts,
    offsets,
    orb,
    grad,
    kron,
    sx,
    poly,
    stage0,
    stage1,
    slab0,
    slab1,
    pack,
    pair_box,
    partner,
    density,
    e_mine,
    e_group,
    e_sum,
    e_row,
    slot_rows,
    slot_of,
    load_sem,
    slot_sem,
    send_sem,
    recv_sem,
):
    me = lax.axis_index("col")
    row = lax.axis_index("row")
    own, edge, plane = orb.shape
    norb = own * n_col
    base = row * norb
    strips = plane // TILE_C
    per_owner = pairs.shape[0]
    mesh_id = pl.DeviceIdType.MESH
    box_stage, slab = (stage0, stage1), (slab0, slab1)

    barrier = pltpu.get_barrier_semaphore()
    side, steps = peers(n_col)

    def peer(step):
        return ((me // side + step[0]) % side) * side + (me % side + step[1]) % side

    for step in steps:
        pl.semaphore_signal(barrier, inc=1, device_id={"col": peer(step)}, device_id_type=mesh_id)

    def greet_row(d, _):
        pl.semaphore_signal(barrier, inc=1, device_id={"row": (row + d) % n_row}, device_id_type=mesh_id)
        return 0

    lax.fori_loop(1, n_row, greet_row, 0)

    sources = (pairs_hbm, counts_hbm, offsets_hbm, orb_hbm, grad_hbm, kron_hbm, sx_hbm, poly_hbm)
    loads = [
        pltpu.make_async_copy(a, b, load_sem.at[i])
        for i, (a, b) in enumerate(zip(sources, (pairs, counts, offsets, orb, grad, kron, sx, poly)))
    ]
    for one in loads[:4]:
        one.start()
    for one in loads[:3]:
        one.wait()

    lane = lax.broadcasted_iota(jnp.int32, (8, TILE_C), 1)

    def place(index, state):
        p, k = index // per_owner, index % per_owner
        at_first = lax.div(pairs[k, 0, p] - base, jnp.int32(own))
        at_second = lax.div(pairs[k, 1, p] - base, jnp.int32(own))
        here = jnp.where(k < counts[p], at_first, -1)
        far = jnp.where(at_first == at_second, -1, here)
        near = jnp.where(at_first == at_second, here, -1)
        out = []
        for device, (count, slots) in zip((far, near), state):
            hit = lane == device
            slots = tuple(jnp.where(hit & (count == s), index, held) for s, held in enumerate(slots))
            out.append((count + hit.astype(jnp.int32), slots))
        return tuple(out)

    none = jnp.full((8, TILE_C), -1, jnp.int32)
    zero = jnp.zeros((8, TILE_C), jnp.int32)
    (far_count, far_slots), (near_count, near_slots) = lax.fori_loop(
        0, n_col * per_owner, place, ((zero, (none,) * REMOTE), (zero, (none,) * LOCAL))
    )
    for s, held in enumerate(far_slots + near_slots):
        slot_rows[pl.ds(s, 1), :] = held[0:1, :]
    over = ((far_count > REMOTE) | (near_count > LOCAL)).astype(jnp.float32)
    overflow = jnp.sum(over[0:1, :], axis=1, keepdims=True)
    to_scalars = pltpu.make_async_copy(slot_rows, slot_of, slot_sem.at[0])
    to_scalars.start()

    def tile_of(s):
        return pl.ds(pl.multiple_of((s // strips) * TILE_R, TILE_R), TILE_R), pl.ds(
            pl.multiple_of((s % strips) * TILE_C, TILE_C), TILE_C
        )

    my_rows, my_cols = tile_of(me)

    def send(src, dst, which, to):
        pltpu.make_async_remote_copy(
            src_ref=src,
            dst_ref=dst,
            send_sem=send_sem.at[which],
            recv_sem=recv_sem.at[which],
            device_id={"col": to},
            device_id_type=mesh_id,
        ).start()

    def arrived(ref, which):
        pltpu.make_async_copy(ref, ref, recv_sem.at[which]).wait()

    def sent(ref, which):
        pltpu.make_async_copy(ref, ref, send_sem.at[which]).wait()

    def send_boxes(r):
        def part(s):
            rows, cols = tile_of(s)
            return box_stage[r].at[:, rows, cols]

        dst = slab[r].at[pl.ds(me * own, own)]
        for step in steps:
            send(part(peer(step)), dst, 2 * r, peer(step))
        pltpu.make_async_copy(part(me), dst, recv_sem.at[2 * r]).start()

    def send_pairs(r):
        dst = pair_box.at[r, :, my_rows, my_cols]

        def fill(to):
            for s in range(REMOTE):
                index = jnp.maximum(slot_of[s, to], 0)
                second = pairs[lax.rem(index, jnp.int32(per_owner)), 1, lax.div(index, jnp.int32(per_owner))]
                pack[r, to, s] = slab[r][jnp.clip(second - base, 0, norb - 1)]

        for step in steps:
            fill(peer(step))
            send(pack.at[r, peer(step)], dst, 2 * r + 1, peer(step))
        fill(me)
        pltpu.make_async_copy(pack.at[r, me], dst, recv_sem.at[2 * r + 1]).start()

    line = lax.broadcasted_iota(jnp.int32, (edge, 1), 0)
    cell = lax.broadcasted_iota(jnp.int32, (1, plane), 1)

    def work(r, start, number, between=None):
        firsts = []
        for n in range(number):
            code = slot_of[start + n, me]
            index = jnp.maximum(code, 0)
            p = lax.div(index, jnp.int32(per_owner))
            k = lax.rem(index, jnp.int32(per_owner))
            first, second = pairs[k, 0, p], pairs[k, 1, p]
            mine = jnp.clip(first - base - me * own, 0, own - 1)
            firsts.append(jnp.where(code >= 0, mine, -1))
            dx = offsets[0, first] - offsets[0, second]
            dy = offsets[1, first] - offsets[1, second]
            dz = offsets[2, first] - offsets[2, second]
            t = dy * edge + dz
            if start < REMOTE:
                moved = pair_box[r, start + n]
            else:
                moved = box_stage[r][jnp.clip(second - base - me * own, 0, own - 1)]
            moved = moved.astype(jnp.float32)
            moved = along_lanes(moved, t)
            moved = pltpu.roll(moved, lax.rem(edge - dx, jnp.int32(edge)), 0)
            at_x = line + dx
            at_y = cell // edge + dy
            at_z = cell % edge + dz
            inside_x = ((at_x >= 0) & (at_x < edge)).astype(jnp.float32)
            inside_yz = ((at_y >= 0) & (at_y < edge) & (at_z >= 0) & (at_z < edge)).astype(jnp.float32)
            moved = moved * inside_yz * inside_x
            partner[pl.ds(n * edge, edge), :] = moved
            density[pl.ds(n * edge, edge), :] = box_stage[r][mine].astype(jnp.float32) * moved
        rows = number * edge

        def halves(x, which):
            high, low = split(x)
            both = dot(jnp.concatenate([high, low], 0), kron[which, 0])
            return both[:rows] + (both[rows:] + dot(high, kron[which, 1]))

        def to_modes(x):
            near, far = x[:, : plane // 2], flipped(x[:, plane // 2 :], edge)
            return jnp.concatenate([halves(near + far, 0), halves(near - far, 1)], 1)

        def to_cells(x):
            even, odd = halves(x[:, : plane // 2], 2), halves(x[:, plane // 2 :], 3)
            return jnp.concatenate([even + odd, flipped(even - odd, edge)], 1)

        def along_x(x):
            out = []
            for n in range(number):
                high, low = split(x[n * edge : (n + 1) * edge])
                out.append(dot(sx[...], jnp.concatenate([high, low, high], 0)))
            return jnp.concatenate(out, 0)

        def energy_of(modes, scaled):
            energy = jnp.zeros((8, TILE_C), jnp.float32)
            for n in range(number):
                part = jnp.sum((modes[n] * scaled[n]).reshape(edge // 8, 8, plane), axis=0)
                part = sum(part[:, c * TILE_C : (c + 1) * TILE_C] for c in range(strips))
                energy = energy + jnp.where(firsts[n] >= 0, part, 0.0)
            return energy

        if between is not None:
            x = density[pl.ds(0, rows), :]
            near, far = x[:, : plane // 2], flipped(x[:, plane // 2 :], edge)
            modes = jnp.concatenate(
                [dot(y.astype(jnp.bfloat16), kron[i, 0]).astype(jnp.bfloat16) for i, y in enumerate((near + far, near - far))], 1
            )
            part = sx[...][:, :edge]
            modes = jnp.stack([dot(part, modes[n * edge : (n + 1) * edge]) for n in range(number)])
            between(energy_of(modes, modes * poly[...][None]))
        modes = along_x(to_modes(density[pl.ds(0, rows), :])).reshape(number, edge, plane)
        scaled = modes * poly[...][None]
        energy = energy_of(modes, scaled) if between is None else None
        potential = to_cells(along_x(scaled.reshape(rows, plane)))
        terms = (potential * partner[pl.ds(0, rows), :]).astype(jnp.bfloat16).astype(jnp.float32)
        for o in range(own):
            total = exchanged[o]
            for n in range(number):
                total = total + jnp.where(firsts[n] == o, terms[n * edge : (n + 1) * edge], 0.0)
            exchanged[o] = total
        return energy

    exchanged[...] = jnp.zeros_like(exchanged)
    loads[3].wait()
    for one in loads[4:]:
        one.start()
    box_stage[0][...] = orb[...].astype(jnp.bfloat16)
    pl.semaphore_wait(barrier, n_col - 1 + n_row - 1)
    send_boxes(0)
    to_scalars.wait()
    for one in loads[4:]:
        one.wait()

    def total_of(energy):
        return jnp.sum(jnp.sum(energy, axis=0, keepdims=True), axis=1, keepdims=True)

    half = LOCAL // 2
    kept = []
    for r in range(ROUNDS):
        energy = work(r, REMOTE, half)
        arrived(slab[r], 2 * r)
        send_pairs(r)
        energy = energy + work(r, REMOTE + half, LOCAL - half)
        arrived(pair_box.at[r], 2 * r + 1)
        if r < ROUNDS - 1:
            kept.append(total_of(energy + work(r, 0, REMOTE)))
            box_stage[r + 1][...] = (orb[...] - damping * ((r + 1.0) * grad[...] + exchanged[...])).astype(jnp.bfloat16)
            send_boxes(r + 1)
        else:

            def send_energy(last):
                values = kept + [total_of(energy + last), overflow]
                at = lax.broadcasted_iota(jnp.int32, (1, TILE_C), 1)
                out = jnp.zeros((1, TILE_C), jnp.float32)
                for i, value in enumerate(values):
                    out = jnp.where(at == i, value, out)
                e_mine[...] = out
                for step in steps:
                    send(e_mine, e_group.at[me], 2 * ROUNDS, peer(step))
                pltpu.make_async_copy(e_mine, e_group.at[me], recv_sem.at[2 * ROUNDS]).start()

            work(r, 0, REMOTE, send_energy)

    orb[...] = orb[...] - damping * (ROUNDS * grad[...] + exchanged[...])
    store = pltpu.make_async_copy(orb, updated_hbm, slot_sem.at[0])
    store.start()

    arrived(e_group, 2 * ROUNDS)
    e_sum[...] = jnp.sum(e_group[...], axis=0)
    last = 2 * ROUNDS + 1

    def go_row(d, _):
        pltpu.make_async_remote_copy(
            src_ref=e_sum,
            dst_ref=e_row.at[row],
            send_sem=send_sem.at[last],
            recv_sem=recv_sem.at[last],
            device_id={"row": (row + d) % n_row},
            device_id_type=mesh_id,
        ).start()
        return 0

    lax.fori_loop(1, n_row, go_row, 0)
    pltpu.make_async_copy(e_sum, e_row.at[row], recv_sem.at[last]).start()
    others = n_col - 1
    for r in range(ROUNDS):
        sent(slab[r].at[pl.ds(0, others * own)], 2 * r)
        sent(pack.at[r, pl.ds(0, others)], 2 * r + 1)
    sent(e_group.at[pl.ds(0, others)], 2 * ROUNDS)
    store.wait()
    arrived(e_row, last)
    values = jnp.sum(e_row[...], axis=0)
    at = lax.broadcasted_iota(jnp.int32, (1, TILE_C), 1)
    for i in range(ROUNDS):
        energy_out[i] = jnp.sum(jnp.where(at == i, values, 0.0)) / (edge * edge * edge * n_row * n_col)
    over_out[0] = jnp.sum(jnp.where(at == ROUNDS, values, 0.0))
    if n_row > 1:
        sent(e_row.at[pl.ds(0, n_row - 1)], last)


def direct_pairs(n_row, n_col, REMOTE, LOCAL, orbitals, gradient, offsets, pairs, counts):
    own, edge, plane = orbitals.shape
    norb = own * n_col
    basis, poly = spectral_tables(edge)
    kron, poly = folded(basis, poly)
    most = max(REMOTE, LOCAL - LOCAL // 2)
    high, low = two_parts(basis)
    sx = np.concatenate([high, high, low], 1)
    smem = pl.BlockSpec(memory_space=pltpu.SMEM)
    f32, bf16 = jnp.float32, jnp.bfloat16
    return pl.pallas_call(
        functools.partial(direct_kernel, n_row, n_col, REMOTE, LOCAL),
        out_shape=(
            jax.ShapeDtypeStruct((own, edge, plane), f32),
            jax.ShapeDtypeStruct((ROUNDS,), f32),
            jax.ShapeDtypeStruct((1,), f32),
        ),
        in_specs=[pl.BlockSpec(memory_space=pl.ANY)] * 8,
        out_specs=(pl.BlockSpec(memory_space=pl.ANY), smem, smem),
        scratch_shapes=[
            pltpu.VMEM((own, edge, plane), f32),
            pltpu.SMEM((pairs.shape[1], 2, n_col), jnp.int32),
            pltpu.SMEM((n_col,), jnp.int32),
            pltpu.SMEM((3, offsets.shape[0]), jnp.int32),
            pltpu.VMEM((own, edge, plane), f32),
            pltpu.VMEM((own, edge, plane), f32),
            pltpu.VMEM((4, 2, plane // 2, plane // 2), bf16),
            pltpu.VMEM((edge, 3 * edge), bf16),
            pltpu.VMEM((edge, plane), f32),
            pltpu.VMEM((own, edge, plane), bf16),
            pltpu.VMEM((own, edge, plane), bf16),
            pltpu.VMEM((norb, TILE_R, TILE_C), bf16),
            pltpu.VMEM((norb, TILE_R, TILE_C), bf16),
            pltpu.VMEM((ROUNDS, n_col, REMOTE, TILE_R, TILE_C), bf16),
            pltpu.VMEM((ROUNDS, REMOTE, edge, plane), bf16),
            pltpu.VMEM((most * edge, plane), f32),
            pltpu.VMEM((most * edge, plane), f32),
            pltpu.VMEM((1, TILE_C), f32),
            pltpu.VMEM((n_col, 1, TILE_C), f32),
            pltpu.VMEM((1, TILE_C), f32),
            pltpu.VMEM((n_row, 1, TILE_C), f32),
            pltpu.VMEM((16, TILE_C), jnp.int32),
            pltpu.SMEM((16, TILE_C), jnp.int32),
            pltpu.SemaphoreType.DMA((8,)),
            pltpu.SemaphoreType.DMA((1,)),
            pltpu.SemaphoreType.DMA((2 * ROUNDS + 2,)),
            pltpu.SemaphoreType.DMA((2 * ROUNDS + 2,)),
        ],
        compiler_params=pltpu.CompilerParams(
            collective_id=1, has_side_effects=True, vmem_limit_bytes=60 * 1024 * 1024
        ),
    )(
        pairs.transpose(1, 2, 0),
        counts,
        offsets.T,
        orbitals,
        gradient,
        jnp.asarray(kron),
        jnp.asarray(sx),
        jnp.asarray(poly.astype(np.float32)),
    )


def local(n_row, n_col, REMOTE, LOCAL, S, orbitals, gradient, offsets, pairs, counts):
    updated, energies, over = direct_pairs(n_row, n_col, REMOTE, LOCAL, orbitals, gradient, offsets, pairs, counts)

    def enough():
        return updated, energies

    def general():
        return spread_pairs(n_row, n_col, S, orbitals, gradient, offsets, pairs, counts)

    return lax.cond(over[0] > 0, general, enough)


def solution(mesh):
    n_row, n_col = mesh.shape["row"], mesh.shape["col"]
    both = P(("row", "col"), None, None)
    return jax.shard_map(
        functools.partial(local, n_row, n_col, 5, 6, 4),
        mesh=mesh,
        in_specs=(both, both, P(), P("row", None, None), P("row")),
        out_specs=(both, P()),
        check_vma=False,
    )
```

```python
import functools

import jax
import jax.numpy as jnp
import ml_dtypes
import numpy as np
from jax import lax
from jax.experimental import pallas as pl
from jax.experimental.pallas import tpu as pltpu
from jax.sharding import PartitionSpec as P

SWEEPS = 12
ROUNDS = 2
TILE_R = 16
TILE_C = 128
screen_mu = 0.1
damping = 0.5


def spectral_tables(edge):
    k = np.arange(1, edge + 1)
    basis = np.sqrt(2.0 / (edge + 1)) * np.sin(np.pi * np.outer(k, k) / (edge + 1))
    line = 2.0 * np.cos(np.pi * k / (edge + 1))
    eig = (6.0 + screen_mu) - (line[:, None, None] + line[None, :, None] + line[None, None, :])
    c, h = 6.0 + screen_mu, 6.0
    g = c / h
    q = 1.0 / g
    u = np.zeros_like(eig)
    t = np.ones_like(eig)
    d = t / c
    for _ in range(SWEEPS):
        u = u + d
        t = t - eig * d
        q_new = 1.0 / (2.0 * g - q)
        d = q_new * q * d + (2.0 * q_new / h) * t
        q = q_new
    return basis, u.reshape(edge, edge * edge)


def two_parts(x):
    high = x.astype(ml_dtypes.bfloat16)
    return np.stack([high, (x - high.astype(np.float64)).astype(ml_dtypes.bfloat16)])


def split(x):
    high = x.astype(jnp.bfloat16)
    return high, (x - high.astype(jnp.float32)).astype(jnp.bfloat16)


def dot(a, b):
    return jnp.dot(a, b, preferred_element_type=jnp.float32)


def dot_split(a, b):
    (a_high, a_low), (b_high, b_low) = a, b
    return dot(a_high, b_high) + (dot(a_low, b_high) + dot(a_high, b_low))


def peers(n_col):
    side = int(round(n_col**0.5))
    steps = [(a, b) for a in range(side) for b in range(side) if a + b > 0]
    return side, sorted(steps, key=lambda p: -(min(p[0], side - p[0]) + min(p[1], side - p[1])))


def spread_kernel(
    n_row,
    n_col,
    S,
    tbl,
    orb_hbm,
    grad_hbm,
    kron_hbm,
    sx_hbm,
    poly_hbm,
    exb,
    energy_out,
    orb,
    grad,
    kron,
    sx,
    poly,
    box_stage,
    q_stage,
    slab0,
    q_slab,
    slab1,
    pack,
    pair_box,
    partner,
    density,
    term_stage,
    terms,
    wide,
    summed,
    final_stage,
    e_mine,
    e_group,
    e_sum,
    e_row,
    first_of,
    second_of,
    load_sem,
    send_sem,
    recv_sem,
):
    me = lax.axis_index("col")
    row = lax.axis_index("row")
    own, edge, plane = orb.shape
    norb = own * n_col
    slots = S * n_col
    halves = edge // TILE_R
    strips = plane // TILE_C

    loads = [
        pltpu.make_async_copy(a, b, load_sem.at[i])
        for i, (a, b) in enumerate(
            ((orb_hbm, orb), (grad_hbm, grad), (kron_hbm, kron), (sx_hbm, sx), (poly_hbm, poly))
        )
    ]
    for one in loads:
        one.start()

    barrier = pltpu.get_barrier_semaphore()

    def greet_col(d, _):
        pl.semaphore_signal(barrier, inc=1, device_id={"col": (me + d) % n_col}, device_id_type=pl.DeviceIdType.MESH)
        return 0

    def greet_row(d, _):
        pl.semaphore_signal(barrier, inc=1, device_id={"row": (row + d) % n_row}, device_id_type=pl.DeviceIdType.MESH)
        return 0

    lax.fori_loop(1, n_col, greet_col, 0)
    lax.fori_loop(1, n_row, greet_row, 0)

    count_at = n_col * 8
    offset_at = count_at + n_col

    def rank(r, firsts):
        def seek(p, state):
            start, found = state
            count = tbl[count_at + p]
            inside = (r >= start) & (r < start + count)
            return start + count, jnp.where(inside, p * 4 + r - start, found)

        total, found = lax.fori_loop(0, n_col, seek, (jnp.int32(0), jnp.int32(-1)))
        at = jnp.maximum(found, 0) * 2
        first = tbl[at]
        first_of[r] = first
        second_of[r] = tbl[at + 1]
        lane = lax.broadcasted_iota(jnp.int32, (norb, slots), 1)
        return jnp.where(lane == r, jnp.where(found >= 0, first, -1), firsts)

    firsts = lax.fori_loop(0, slots, rank, jnp.full((norb, slots), -1, jnp.int32))
    choose = (lax.broadcasted_iota(jnp.int32, (norb, slots), 0) == firsts).astype(jnp.float32).astype(jnp.bfloat16)

    def total_live(p, acc):
        return acc + tbl[count_at + p]

    live_total = lax.fori_loop(0, n_col, total_live, jnp.int32(0))

    def tile_of(s):
        return pl.ds(pl.multiple_of((s // strips) * TILE_R, TILE_R), TILE_R), pl.ds(
            pl.multiple_of((s % strips) * TILE_C, TILE_C), TILE_C
        )

    my_rows, my_cols = tile_of(me)

    def exchange(src_of, dst, which, before=None):
        side, steps = peers(n_col)
        for dy, dz in steps:
            to = ((me // side + dy) % side) * side + (me % side + dz) % side
            if before is not None:
                before(to)
            pltpu.make_async_remote_copy(
                src_ref=src_of(to),
                dst_ref=dst,
                send_sem=send_sem.at[which],
                recv_sem=recv_sem.at[which],
                device_id={"col": to},
                device_id_type=pl.DeviceIdType.MESH,
            ).start()
        if before is not None:
            before(me)
        pltpu.make_async_copy(src_of(me), dst, recv_sem.at[which]).start()

    def arrived(ref, which):
        pltpu.make_async_copy(ref, ref, recv_sem.at[which]).wait()

    def sent(ref, which):
        pltpu.make_async_copy(ref, ref, send_sem.at[which]).wait()

    loads[0].wait()
    box_stage[...] = orb[...].astype(jnp.bfloat16)
    pl.semaphore_wait(barrier, n_col - 1 + n_row - 1)

    def from_boxes(s):
        rows, cols = tile_of(s)
        return box_stage.at[:, rows, cols]

    def from_q(s):
        rows, cols = tile_of(s)
        return q_stage.at[:, rows, cols]

    mine4 = pl.ds(me * own, own)
    exchange(from_boxes, slab0.at[mine4], 0)
    loads[1].wait()
    q_stage[...] = orb[...] - damping * grad[...]
    exchange(from_q, q_slab.at[mine4], 1)
    for one in loads[2:]:
        one.wait()

    energies = []
    for r in range(ROUNDS):
        slab = (slab0, slab1)[r]
        if r == 0:
            arrived(slab0, 0)

        def fill(p):
            for k in range(S):
                pack[r, p * 2 * S + 2 * k] = slab[first_of[p * S + k]]
                pack[r, p * 2 * S + 2 * k + 1] = slab[second_of[p * S + k]]

        def from_pack(p):
            return pack.at[r, pl.ds(p * 2 * S, 2 * S)]

        exchange(from_pack, pair_box.at[r, :, my_rows, my_cols], 2 + 2 * r, fill)
        arrived(pair_box.at[r], 2 + 2 * r)

        lane = lax.broadcasted_iota(jnp.int32, (edge, plane), 1)
        line = lax.broadcasted_iota(jnp.int32, (edge, plane), 0)
        for k in range(S):
            a = offset_at + 3 * first_of[me * S + k]
            b = offset_at + 3 * second_of[me * S + k]
            dx = tbl[a] - tbl[b]
            dy = tbl[a + 1] - tbl[b + 1]
            dz = tbl[a + 2] - tbl[b + 2]
            t = dy * edge + dz
            moved = pair_box[r, 2 * k + 1].astype(jnp.float32)
            moved = pltpu.roll(moved, lax.rem(plane - t, jnp.int32(plane)), 1)
            moved = pltpu.roll(moved, lax.rem(edge - dx, jnp.int32(edge)), 0)
            at_x = line + dx
            at_y = lane // edge + dy
            at_z = lane % edge + dz
            inside = (
                (at_x >= 0) & (at_x < edge) & (at_y >= 0) & (at_y < edge) & (at_z >= 0) & (at_z < edge)
            )
            moved = jnp.where(inside, moved, 0.0)
            partner[pl.ds(k * edge, edge), :] = moved
            density[pl.ds(k * edge, edge), :] = pair_box[r, 2 * k].astype(jnp.float32) * moved

        yz = kron[0], kron[1]
        along_x = sx[0], sx[1]
        modes = dot_split(split(density[...]), yz)
        modes = dot_split(along_x, split(modes)).reshape(S, edge, plane) * poly[...][None]
        modes = dot_split(along_x, split(modes.reshape(S * edge, plane)))
        potential = dot_split(split(modes), yz)
        term_stage[r] = (potential * partner[...]).astype(jnp.bfloat16).reshape(S, edge, plane)
        cells = (density[...] * potential).reshape(S, edge, plane)
        energy = jnp.zeros((edge, plane), jnp.float32)
        for k in range(S):
            energy = energy + jnp.where(me * S + k < live_total, cells[k], 0.0)
        energies.append(energy)

        def from_terms(s):
            rows, cols = tile_of(s)
            return term_stage.at[r, :, rows, cols]

        exchange(from_terms, terms.at[r, pl.ds(me * S, S)], 3 + 2 * r)

        if r == ROUNDS - 1:
            for i, e in enumerate(energies):
                part = jnp.sum(e.reshape(edge // 8, 8, plane), axis=0)
                e_mine[i] = sum(part[:, c * TILE_C : (c + 1) * TILE_C] for c in range(strips))
            exchange(lambda s: e_mine, e_group.at[me], 7)

        arrived(terms.at[r], 3 + 2 * r)
        wide[...] = terms[r].astype(jnp.float32).reshape(slots * TILE_R, TILE_C)
        if r == 0:
            arrived(q_slab, 1)
        for j in range(TILE_R):
            part = wide[pl.ds(j, slots, stride=TILE_R), :].astype(jnp.bfloat16)
            out = dot(choose, part)
            if r == 0:
                summed[pl.ds(j, norb, stride=TILE_R), :] = out
            else:
                summed[pl.ds(j, norb, stride=TILE_R), :] += out
        if r == 0:
            total = summed[...].reshape(norb, TILE_R, TILE_C)
            slab1[...] = (q_slab[...] - damping * total).astype(jnp.bfloat16)
        else:
            final_stage[...] = summed[...].reshape(norb, TILE_R, TILE_C).astype(jnp.bfloat16)

    exchange(lambda s: final_stage.at[pl.ds(s * own, own)], exb.at[:, my_rows, my_cols], 6)

    arrived(e_group, 7)
    e_sum[...] = jnp.sum(e_group[...], axis=0)

    def go_row(d, _):
        pltpu.make_async_remote_copy(
            src_ref=e_sum,
            dst_ref=e_row.at[row],
            send_sem=send_sem.at[8],
            recv_sem=recv_sem.at[8],
            device_id={"row": (row + d) % n_row},
            device_id_type=pl.DeviceIdType.MESH,
        ).start()
        return 0

    lax.fori_loop(1, n_row, go_row, 0)
    pltpu.make_async_copy(e_sum, e_row.at[row], recv_sem.at[8]).start()
    arrived(e_row, 8)
    all_cells = edge * edge * edge * n_row * n_col
    for i in range(ROUNDS):
        energy_out[i] = jnp.sum(jnp.sum(e_row[:, i], axis=0)) / all_cells
    arrived(exb, 6)

    others = n_col - 1
    sent(slab0.at[pl.ds(0, others * own)], 0)
    sent(q_slab.at[pl.ds(0, others * own)], 1)
    for r in range(ROUNDS):
        sent(pack.at[r, pl.ds(0, others * 2 * S)], 2 + 2 * r)
        sent(terms.at[r, pl.ds(0, others * S)], 3 + 2 * r)
    sent(final_stage.at[pl.ds(0, others * own)], 6)
    sent(e_group.at[pl.ds(0, others)], 7)
    if n_row > 1:
        sent(e_row.at[pl.ds(0, n_row - 1)], 8)


def spread_pairs(n_row, n_col, S, orbitals, gradient, offsets, pairs, counts):
    own, edge, plane = orbitals.shape
    norb = own * n_col
    slots = S * n_col
    base = lax.axis_index("row") * norb
    table = jnp.concatenate(
        [
            (pairs - base).reshape(-1),
            counts,
            lax.dynamic_slice_in_dim(offsets, base, norb, 0).reshape(-1),
        ]
    )
    basis, poly = spectral_tables(edge)
    kron = two_parts(np.kron(basis, basis))
    sx = two_parts(np.kron(np.eye(S), basis))
    hbm = pl.BlockSpec(memory_space=pltpu.HBM)
    f32, bf16 = jnp.float32, jnp.bfloat16
    tiles = (norb, TILE_R, TILE_C)
    exchanged, energies = pl.pallas_call(
        functools.partial(spread_kernel, n_row, n_col, S),
        out_shape=(
            jax.ShapeDtypeStruct((own, edge, plane), bf16),
            jax.ShapeDtypeStruct((ROUNDS,), f32),
        ),
        in_specs=[pl.BlockSpec(memory_space=pltpu.SMEM)] + [hbm] * 5,
        out_specs=(pl.BlockSpec(memory_space=pltpu.VMEM), pl.BlockSpec(memory_space=pltpu.SMEM)),
        scratch_shapes=[
            pltpu.VMEM((own, edge, plane), f32),
            pltpu.VMEM((own, edge, plane), f32),
            pltpu.VMEM((2, plane, plane), bf16),
            pltpu.VMEM((2, S * edge, S * edge), bf16),
            pltpu.VMEM((edge, plane), f32),
            pltpu.VMEM((own, edge, plane), bf16),
            pltpu.VMEM((own, edge, plane), f32),
            pltpu.VMEM(tiles, bf16),
            pltpu.VMEM(tiles, f32),
            pltpu.VMEM(tiles, bf16),
            pltpu.VMEM((ROUNDS, slots * 2, TILE_R, TILE_C), bf16),
            pltpu.VMEM((ROUNDS, 2 * S, edge, plane), bf16),
            pltpu.VMEM((S * edge, plane), f32),
            pltpu.VMEM((S * edge, plane), f32),
            pltpu.VMEM((ROUNDS, S, edge, plane), bf16),
            pltpu.VMEM((ROUNDS, slots, TILE_R, TILE_C), bf16),
            pltpu.VMEM((slots * TILE_R, TILE_C), f32),
            pltpu.VMEM((norb * TILE_R, TILE_C), f32),
            pltpu.VMEM(tiles, bf16),
            pltpu.VMEM((ROUNDS, 8, TILE_C), f32),
            pltpu.VMEM((n_col, ROUNDS, 8, TILE_C), f32),
            pltpu.VMEM((ROUNDS, 8, TILE_C), f32),
            pltpu.VMEM((n_row, ROUNDS, 8, TILE_C), f32),
            pltpu.SMEM((slots,), jnp.int32),
            pltpu.SMEM((slots,), jnp.int32),
            pltpu.SemaphoreType.DMA((5,)),
            pltpu.SemaphoreType.DMA((9,)),
            pltpu.SemaphoreType.DMA((9,)),
        ],
        compiler_params=pltpu.CompilerParams(
            collective_id=S, has_side_effects=True, vmem_limit_bytes=60 * 1024 * 1024
        ),
    )(table, orbitals, gradient, jnp.asarray(kron), jnp.asarray(sx), jnp.asarray(poly.astype(np.float32)))
    updated = orbitals - gradient - damping * exchanged.astype(f32)
    return updated, energies


def flipped(x, edge):
    per_tile = TILE_C // edge
    tiles = x.shape[1] // TILE_C
    block = lax.broadcasted_iota(jnp.int32, (1, TILE_C), 1) // edge
    out = []
    for t in reversed(range(tiles)):
        tile = x[:, t * TILE_C : (t + 1) * TILE_C]
        step = per_tile // 2
        while step:
            back = pltpu.roll(tile, TILE_C - step * edge, 1)
            if 2 * step == per_tile:
                tile = back
            else:
                ahead = pltpu.roll(tile, step * edge, 1)
                tile = jnp.where(block // step % 2 == 0, back, ahead)
            step //= 2
        out.append(tile)
    return jnp.concatenate(out, 1)


def folded(basis, poly):
    edge = basis.shape[0]
    half = [np.kron(basis[i::2, : edge // 2].T, basis) for i in range(2)]
    kron = np.stack([two_parts(x) for x in half + [x.T for x in half]])
    poly = poly.reshape(edge, edge, edge)
    poly = np.concatenate([poly[:, 0::2], poly[:, 1::2]], 1)
    return kron, poly.reshape(edge, edge * edge)


def along_lanes(x, step):
    tiles = x.shape[1] // TILE_C
    left = step < 0
    turn = jnp.where(left, step + TILE_C, step)
    lane = lax.broadcasted_iota(jnp.int32, (1, TILE_C), 1)
    own = lane < TILE_C - turn
    back = lax.rem(TILE_C - turn, jnp.int32(TILE_C))
    turned = [pltpu.roll(x[:, t * TILE_C : (t + 1) * TILE_C], back, 1) for t in range(tiles)]
    before = own & left
    after = jnp.logical_not(own | left)
    out = []
    for t in range(tiles):
        tile = turned[t]
        tile = jnp.where(before, turned[t - 1], tile) if t > 0 else tile
        out.append(jnp.where(after, turned[t + 1], tile) if t < tiles - 1 else tile)
    return jnp.concatenate(out, 1)


def direct_kernel(
    n_row,
    n_col,
    REMOTE,
    LOCAL,
    pairs_hbm,
    counts_hbm,
    offsets_hbm,
    orb_hbm,
    grad_hbm,
    kron_hbm,
    sx_hbm,
    poly_hbm,
    updated_hbm,
    energy_out,
    over_out,
    exchanged,
    pairs,
    counts,
    offsets,
    orb,
    grad,
    kron,
    sx,
    poly,
    stage0,
    stage1,
    slab0,
    slab1,
    pack,
    pair_box,
    partner,
    density,
    e_mine,
    e_group,
    e_sum,
    e_row,
    slot_rows,
    slot_of,
    held,
    inside_yz,
    load_sem,
    slot_sem,
    send_sem,
    recv_sem,
):
    me = lax.axis_index("col")
    row = lax.axis_index("row")
    own, edge, plane = orb.shape
    norb = own * n_col
    base = row * norb
    strips = plane // TILE_C
    per_owner = pairs.shape[0]
    mesh_id = pl.DeviceIdType.MESH
    box_stage, slab = (stage0, stage1), (slab0, slab1)

    barrier = pltpu.get_barrier_semaphore()
    side, steps = peers(n_col)

    def peer(step):
        return ((me // side + step[0]) % side) * side + (me % side + step[1]) % side

    for step in steps:
        pl.semaphore_signal(barrier, inc=1, device_id={"col": peer(step)}, device_id_type=mesh_id)

    def greet_row(d, _):
        pl.semaphore_signal(barrier, inc=1, device_id={"row": (row + d) % n_row}, device_id_type=mesh_id)
        return 0

    lax.fori_loop(1, n_row, greet_row, 0)

    sources = (pairs_hbm, counts_hbm, offsets_hbm, orb_hbm, grad_hbm, kron_hbm, sx_hbm, poly_hbm)
    loads = [
        pltpu.make_async_copy(a, b, load_sem.at[i])
        for i, (a, b) in enumerate(zip(sources, (pairs, counts, offsets, orb, grad, kron, sx, poly)))
    ]
    for one in loads[:4]:
        one.start()
    for one in loads[:3]:
        one.wait()

    lane = lax.broadcasted_iota(jnp.int32, (8, TILE_C), 1)

    def place(index, state):
        p, k = index // per_owner, index % per_owner
        at_first = lax.div(pairs[k, 0, p] - base, jnp.int32(own))
        second = jnp.clip(pairs[k, 1, p] - base, 0, norb - 1)
        at_second = lax.div(second, jnp.int32(own))
        here = jnp.where(k < counts[p], at_first, -1)
        far = jnp.where(at_first == at_second, -1, here)
        near = jnp.where(at_first == at_second, here, -1)
        far_count, far_slots, far_seconds, near_count, near_slots = state
        hit = lane == far
        here = [hit & (far_count == s) for s in range(REMOTE)]
        far_slots = tuple(jnp.where(at, index, was) for at, was in zip(here, far_slots))
        far_seconds = tuple(jnp.where(at, second, was) for at, was in zip(here, far_seconds))
        far_count = far_count + hit.astype(jnp.int32)
        hit = lane == near
        near_slots = tuple(jnp.where(hit & (near_count == s), index, was) for s, was in enumerate(near_slots))
        return far_count, far_slots, far_seconds, near_count + hit.astype(jnp.int32), near_slots

    none = jnp.full((8, TILE_C), -1, jnp.int32)
    zero = jnp.zeros((8, TILE_C), jnp.int32)
    far_count, far_slots, far_seconds, near_count, near_slots = lax.fori_loop(
        0, n_col * per_owner, place, (zero, (none,) * REMOTE, (zero,) * REMOTE, zero, (none,) * LOCAL)
    )
    for s, entry in enumerate(far_slots + near_slots + far_seconds):
        slot_rows[pl.ds(s, 1), :] = entry[0:1, :]
    over = ((far_count > REMOTE) | (near_count > LOCAL)).astype(jnp.float32)
    overflow = jnp.sum(over[0:1, :], axis=1, keepdims=True)
    to_scalars = pltpu.make_async_copy(slot_rows, slot_of, slot_sem.at[0])
    to_scalars.start()

    def tile_of(s):
        return pl.ds(pl.multiple_of((s // strips) * TILE_R, TILE_R), TILE_R), pl.ds(
            pl.multiple_of((s % strips) * TILE_C, TILE_C), TILE_C
        )

    my_rows, my_cols = tile_of(me)

    def send(src, dst, which, to):
        pltpu.make_async_remote_copy(
            src_ref=src,
            dst_ref=dst,
            send_sem=send_sem.at[which],
            recv_sem=recv_sem.at[which],
            device_id={"col": to},
            device_id_type=mesh_id,
        ).start()

    def arrived(ref, which):
        pltpu.make_async_copy(ref, ref, recv_sem.at[which]).wait()

    def sent(ref, which):
        pltpu.make_async_copy(ref, ref, send_sem.at[which]).wait()

    def send_boxes(r):
        def part(s):
            rows, cols = tile_of(s)
            return box_stage[r].at[:, rows, cols]

        dst = slab[r].at[pl.ds(me * own, own)]
        for step in steps:
            send(part(peer(step)), dst, 2 * r, peer(step))
        pltpu.make_async_copy(part(me), dst, recv_sem.at[2 * r]).start()

    def send_pairs(r):
        dst = pair_box.at[r, :, my_rows, my_cols]

        def fill(to):
            for s in range(REMOTE):
                pack[r, to, s] = slab[r][slot_of[REMOTE + LOCAL + s, to]]

        for step in steps:
            fill(peer(step))
            send(pack.at[r, peer(step)], dst, 2 * r + 1, peer(step))
        fill(me)
        pltpu.make_async_copy(pack.at[r, me], dst, recv_sem.at[2 * r + 1]).start()

    line = lax.broadcasted_iota(jnp.int32, (edge, 1), 0)
    cell = lax.broadcasted_iota(jnp.int32, (1, plane), 1)

    def work(r, start, number, between=None):
        firsts = []
        for n in range(number):
            live, mine, other, t, dx = facts[start + n]
            firsts.append(live)
            if start < REMOTE:
                moved = pair_box[r, start + n]
            else:
                moved = box_stage[r][other]
            moved = moved.astype(jnp.float32)
            moved = along_lanes(moved, t)
            moved = pltpu.roll(moved, lax.rem(edge - dx, jnp.int32(edge)), 0)
            inside_x = ((line + dx >= 0) & (line + dx < edge)).astype(jnp.float32)
            moved = moved * inside_yz[start + n] * inside_x
            partner[pl.ds(n * edge, edge), :] = moved
            density[pl.ds(n * edge, edge), :] = box_stage[r][mine].astype(jnp.float32) * moved
        rows = number * edge

        def halves(x, which):
            high, low = split(x)
            both = dot(jnp.concatenate([high, low], 0), kron[which, 0])
            return both[:rows] + (both[rows:] + dot(high, kron[which, 1]))

        def to_modes(x):
            near, far = x[:, : plane // 2], flipped(x[:, plane // 2 :], edge)
            return jnp.concatenate([halves(near + far, 0), halves(near - far, 1)], 1)

        def to_cells(x):
            even, odd = halves(x[:, : plane // 2], 2), halves(x[:, plane // 2 :], 3)
            return jnp.concatenate([even + odd, flipped(even - odd, edge)], 1)

        def along_x(x):
            high, low = split(x)
            part = sx[0, pl.ds(0, rows), pl.ds(0, rows)]
            both = dot(jnp.concatenate([part, sx[1, pl.ds(0, rows), pl.ds(0, rows)]], 0), high)
            return both[:rows] + (both[rows:] + dot(part, low))

        def energy_of(modes, scaled):
            energy = jnp.zeros((8, TILE_C), jnp.float32)
            for n in range(number):
                part = jnp.sum((modes[n] * scaled[n]).reshape(edge // 8, 8, plane), axis=0)
                part = sum(part[:, c * TILE_C : (c + 1) * TILE_C] for c in range(strips))
                energy = energy + jnp.where(firsts[n] >= 0, part, 0.0)
            return energy

        if between is not None:
            x = density[pl.ds(0, rows), :]
            near, far = x[:, : plane // 2], flipped(x[:, plane // 2 :], edge)
            modes = jnp.concatenate(
                [dot(y.astype(jnp.bfloat16), kron[i, 0]).astype(jnp.bfloat16) for i, y in enumerate((near + far, near - far))], 1
            )
            modes = dot(sx[0, pl.ds(0, rows), pl.ds(0, rows)], modes).reshape(number, edge, plane)
            between(energy_of(modes, modes * poly[...][None]))
        modes = along_x(to_modes(density[pl.ds(0, rows), :])).reshape(number, edge, plane)
        scaled = modes * poly[...][None]
        energy = energy_of(modes, scaled) if between is None else None
        potential = to_cells(along_x(scaled.reshape(rows, plane)))
        terms = (potential * partner[pl.ds(0, rows), :]).astype(jnp.bfloat16).astype(jnp.float32)
        for o in range(own):
            total = exchanged[o]
            for n in range(number):
                total = total + jnp.where(firsts[n] == o, terms[n * edge : (n + 1) * edge], 0.0)
            exchanged[o] = total
        return energy

    exchanged[...] = jnp.zeros_like(exchanged)
    loads[3].wait()
    for one in loads[4:]:
        one.start()
    box_stage[0][...] = orb[...].astype(jnp.bfloat16)
    pl.semaphore_wait(barrier, n_col - 1 + n_row - 1)
    send_boxes(0)
    to_scalars.wait()
    for one in loads[4:]:
        one.wait()

    facts = []
    for slot in range(REMOTE + LOCAL):
        code = slot_of[slot, me]
        index = jnp.maximum(code, 0)
        p, k = lax.div(index, jnp.int32(per_owner)), lax.rem(index, jnp.int32(per_owner))
        first, second = pairs[k, 0, p], pairs[k, 1, p]
        mine = jnp.clip(first - base - me * own, 0, own - 1)
        other = jnp.clip(second - base - me * own, 0, own - 1)
        dx = offsets[0, first] - offsets[0, second]
        dy = offsets[1, first] - offsets[1, second]
        dz = offsets[2, first] - offsets[2, second]
        at_y, at_z = cell // edge + dy, cell % edge + dz
        inside = (at_y >= 0) & (at_y < edge) & (at_z >= 0) & (at_z < edge)
        inside_yz[slot] = inside.astype(jnp.float32)
        facts.append((jnp.where(code >= 0, mine, -1), mine, other, dy * edge + dz, dx))
    held[...] = orb[...] - damping * grad[...]

    def total_of(energy):
        return jnp.sum(jnp.sum(energy, axis=0, keepdims=True), axis=1, keepdims=True)

    half = LOCAL // 2
    kept = []
    for r in range(ROUNDS):
        energy = work(r, REMOTE, half)
        arrived(slab[r], 2 * r)
        send_pairs(r)
        energy = energy + work(r, REMOTE + half, LOCAL - half)
        arrived(pair_box.at[r], 2 * r + 1)
        if r < ROUNDS - 1:
            kept.append(total_of(energy + work(r, 0, REMOTE)))
            box_stage[r + 1][...] = (held[...] - damping * exchanged[...]).astype(jnp.bfloat16)
            send_boxes(r + 1)
        else:

            def send_energy(last):
                values = kept + [total_of(energy + last), overflow]
                at = lax.broadcasted_iota(jnp.int32, (1, TILE_C), 1)
                out = jnp.zeros((1, TILE_C), jnp.float32)
                for i, value in enumerate(values):
                    out = jnp.where(at == i, value, out)
                e_mine[...] = out
                for step in steps:
                    send(e_mine, e_group.at[me], 2 * ROUNDS, peer(step))
                pltpu.make_async_copy(e_mine, e_group.at[me], recv_sem.at[2 * ROUNDS]).start()

            work(r, 0, REMOTE, send_energy)

    orb[...] = orb[...] - damping * (ROUNDS * grad[...] + exchanged[...])
    store = pltpu.make_async_copy(orb, updated_hbm, slot_sem.at[0])
    store.start()

    arrived(e_group, 2 * ROUNDS)
    e_sum[...] = jnp.sum(e_group[...], axis=0)
    last = 2 * ROUNDS + 1

    def go_row(d, _):
        pltpu.make_async_remote_copy(
            src_ref=e_sum,
            dst_ref=e_row.at[row],
            send_sem=send_sem.at[last],
            recv_sem=recv_sem.at[last],
            device_id={"row": (row + d) % n_row},
            device_id_type=mesh_id,
        ).start()
        return 0

    lax.fori_loop(1, n_row, go_row, 0)
    pltpu.make_async_copy(e_sum, e_row.at[row], recv_sem.at[last]).start()
    others = n_col - 1
    for r in range(ROUNDS):
        sent(slab[r].at[pl.ds(0, others * own)], 2 * r)
        sent(pack.at[r, pl.ds(0, others)], 2 * r + 1)
    sent(e_group.at[pl.ds(0, others)], 2 * ROUNDS)
    store.wait()
    arrived(e_row, last)
    values = jnp.sum(e_row[...], axis=0)
    at = lax.broadcasted_iota(jnp.int32, (1, TILE_C), 1)
    for i in range(ROUNDS):
        energy_out[i] = jnp.sum(jnp.where(at == i, values, 0.0)) / (edge * edge * edge * n_row * n_col)
    over_out[0] = jnp.sum(jnp.where(at == ROUNDS, values, 0.0))
    if n_row > 1:
        sent(e_row.at[pl.ds(0, n_row - 1)], last)


def direct_pairs(n_row, n_col, REMOTE, LOCAL, orbitals, gradient, offsets, pairs, counts):
    own, edge, plane = orbitals.shape
    norb = own * n_col
    basis, poly = spectral_tables(edge)
    kron, poly = folded(basis, poly)
    most = max(REMOTE, LOCAL - LOCAL // 2)
    sx = two_parts(np.kron(np.eye(most), basis))
    smem = pl.BlockSpec(memory_space=pltpu.SMEM)
    f32, bf16 = jnp.float32, jnp.bfloat16
    return pl.pallas_call(
        functools.partial(direct_kernel, n_row, n_col, REMOTE, LOCAL),
        out_shape=(
            jax.ShapeDtypeStruct((own, edge, plane), f32),
            jax.ShapeDtypeStruct((ROUNDS,), f32),
            jax.ShapeDtypeStruct((1,), f32),
        ),
        in_specs=[pl.BlockSpec(memory_space=pl.ANY)] * 8,
        out_specs=(pl.BlockSpec(memory_space=pl.ANY), smem, smem),
        scratch_shapes=[
            pltpu.VMEM((own, edge, plane), f32),
            pltpu.SMEM((pairs.shape[1], 2, n_col), jnp.int32),
            pltpu.SMEM((n_col,), jnp.int32),
            pltpu.SMEM((3, offsets.shape[0]), jnp.int32),
            pltpu.VMEM((own, edge, plane), f32),
            pltpu.VMEM((own, edge, plane), f32),
            pltpu.VMEM((4, 2, plane // 2, plane // 2), bf16),
            pltpu.VMEM((2, most * edge, most * edge), bf16),
            pltpu.VMEM((edge, plane), f32),
            pltpu.VMEM((own, edge, plane), bf16),
            pltpu.VMEM((own, edge, plane), bf16),
            pltpu.VMEM((norb, TILE_R, TILE_C), bf16),
            pltpu.VMEM((norb, TILE_R, TILE_C), bf16),
            pltpu.VMEM((ROUNDS, n_col, REMOTE, TILE_R, TILE_C), bf16),
            pltpu.VMEM((ROUNDS, REMOTE, edge, plane), bf16),
            pltpu.VMEM((most * edge, plane), f32),
            pltpu.VMEM((most * edge, plane), f32),
            pltpu.VMEM((1, TILE_C), f32),
            pltpu.VMEM((n_col, 1, TILE_C), f32),
            pltpu.VMEM((1, TILE_C), f32),
            pltpu.VMEM((n_row, 1, TILE_C), f32),
            pltpu.VMEM((-(-(2 * REMOTE + LOCAL) // 8) * 8, TILE_C), jnp.int32),
            pltpu.SMEM((-(-(2 * REMOTE + LOCAL) // 8) * 8, TILE_C), jnp.int32),
            pltpu.VMEM((own, edge, plane), f32),
            pltpu.VMEM((REMOTE + LOCAL, 1, plane), f32),
            pltpu.SemaphoreType.DMA((8,)),
            pltpu.SemaphoreType.DMA((1,)),
            pltpu.SemaphoreType.DMA((2 * ROUNDS + 2,)),
            pltpu.SemaphoreType.DMA((2 * ROUNDS + 2,)),
        ],
        compiler_params=pltpu.CompilerParams(
            collective_id=1, has_side_effects=True, vmem_limit_bytes=60 * 1024 * 1024
        ),
    )(
        pairs.transpose(1, 2, 0),
        counts,
        offsets.T,
        orbitals,
        gradient,
        jnp.asarray(kron),
        jnp.asarray(sx),
        jnp.asarray(poly.astype(np.float32)),
    )


def local(n_row, n_col, REMOTE, LOCAL, S, orbitals, gradient, offsets, pairs, counts):
    updated, energies, over = direct_pairs(n_row, n_col, REMOTE, LOCAL, orbitals, gradient, offsets, pairs, counts)

    def enough():
        return updated, energies

    def general():
        return spread_pairs(n_row, n_col, S, orbitals, gradient, offsets, pairs, counts)

    return lax.cond(over[0] > 0, general, enough)


def solution(mesh):
    n_row, n_col = mesh.shape["row"], mesh.shape["col"]
    both = P(("row", "col"), None, None)
    return jax.shard_map(
        functools.partial(local, n_row, n_col, 5, 6, 4),
        mesh=mesh,
        in_specs=(both, both, P(), P("row", None, None), P("row")),
        out_specs=(both, P()),
        check_vma=False,
    )
```
